32 devices in a mesh: row: 4 (over z), col: 4 (over x, core), layer: 2 (over y).
Axes of the slice: x: 2, y: 2, z: 4, core: 2. Of those that a mesh axis runs over, the one named last changes fastest.
Arguments:
- density: bfloat16 [64, 11, 128, 128], P(('row', 'layer'), None, 'col'), may hold values from -1.5 to 1.5, as said below
- pattern: int32 [64, 11], replicated, may hold values from -1 to 63, as said below
- square_filter: int32 [64, 12], replicated, may hold values from 0 to 63, as said below
- cube_filter: int32 [64, 16], replicated, may hold values from 0 to 63, as said below
Outputs:
- purified: float32 [64, 16, 128, 128], P(('row', 'layer'), 'col')
The draws below stay inside these ranges and needn't reach their ends.
Inputs may be any that keep to these rules, and one draw needn't show every extreme that they name: `density`: slot s of block row i holds the block of P at (i, pattern[i, s]), and zeros where pattern[i, s] is -1; the matrix so described is exactly symmetric. Row i lists distinct block columns, each within 5 of i modulo 64, i itself among them; unused slots hold -1; the block pattern is symmetric; some block row uses all 11 slots. `square_filter`: row i lists 12 distinct block columns, each within 10 of i modulo 64. `cube_filter`: row i lists 16 distinct block columns, each within 15 of i modulo 64.
All inputs are finite; a program needn't handle non-finite values.
Results may differ from the reference program's by a relative error of at most 0.0023.
Values may be sent and summed in bfloat16 or wider, within the bound.
No kernel may reach another device: no remote copies, remote signals or barrier semaphores. Data moves between devices by JAX's collectives and lax.ppermute only.
A program may use at most 64 MiB of HBM per device.

```python
import jax
import jax.numpy as jnp
from jax import lax

BLOCK = 128
RADIUS = 5
SLOTS = 11
SQ_SLOTS = 12
CUBE_SLOTS = 16
NB = 64


def live_band(key):
    coins = jax.random.randint(jax.random.fold_in(key, 41), (NB, RADIUS), 0, 10) < 7
    full_row = jax.random.randint(jax.random.fold_in(key, 42), (), 0, NB)
    rows = jnp.arange(NB)
    steps = jnp.arange(1, RADIUS + 1)
    edges = coins | (rows[:, None] == full_row) | (rows[:, None] == (full_row - steps[None, :]) % NB)
    offsets = jnp.arange(SLOTS) - RADIUS
    base = jnp.where(offsets[None, :] > 0, rows[:, None], (rows[:, None] + offsets[None, :]) % NB)
    gap = jnp.clip(jnp.abs(offsets) - 1, 0, RADIUS - 1)
    live = jnp.where(offsets[None, :] == 0, True, edges[base, gap[None, :]])
    ranks = jnp.where(live, 0, SLOTS) + jnp.arange(SLOTS)[None, :]
    order = jnp.argsort(ranks, axis=1, stable=True)
    return (live, base, gap, offsets, order)


def draw_pattern(key, part):
    live, base, gap, offsets, order = live_band(jax.random.fold_in(key, 40))
    rows = jnp.arange(NB)
    columns = jnp.where(live, (rows[:, None] + offsets[None, :]) % NB, -1)
    return jnp.take_along_axis(columns, order, axis=1).astype(jnp.int32)


def draw_density(key, part):
    live, base, gap, offsets, order = live_band(jax.random.fold_in(key, 40))
    noise_key = jax.random.fold_in(key, 51)
    diag_key = jax.random.fold_in(key, 52)
    pair_noise = 0.08 * jnp.clip(jax.random.normal(noise_key, (NB, RADIUS, BLOCK, BLOCK), jnp.float32), -4.0, 4.0)
    diag_noise = 0.08 * jnp.clip(jax.random.normal(diag_key, (NB, BLOCK, BLOCK), jnp.float32), -4.0, 4.0)
    identity = (jnp.arange(BLOCK)[:, None] == jnp.arange(BLOCK)[None, :]).astype(jnp.float32)
    diag_block = 0.5 * identity[None] + 0.7071 * (diag_noise + jnp.swapaxes(diag_noise, 1, 2))
    picked = pair_noise[base, gap[None, :]]
    flipped = jnp.swapaxes(picked, 2, 3)
    band = jnp.where(offsets[None, :, None, None] < 0, flipped, picked)
    band = jnp.where(offsets[None, :, None, None] == 0, diag_block[:, None], band)
    band = band * live[:, :, None, None].astype(jnp.float32)
    return jnp.take_along_axis(band, order[:, :, None, None], axis=1).astype(jnp.bfloat16)


def window_filter(key, reach, keep):
    width = 2 * reach + 1
    scores = jax.random.randint(key, (NB, width), 0, 1 << 20) * width + jnp.arange(width)[None, :]
    chosen = jnp.argsort(scores, axis=1, stable=True)[:, :keep]
    return ((jnp.arange(NB)[:, None] + chosen - reach) % NB).astype(jnp.int32)


def draw_square_filter(key, part):
    return window_filter(jax.random.fold_in(key, 61), 2 * RADIUS, SQ_SLOTS)


def draw_cube_filter(key, part):
    return window_filter(jax.random.fold_in(key, 71), 3 * RADIUS, CUBE_SLOTS)


def setup_inputs(seed: int = 0) -> dict:
    arg_keys = jax.random.split(jax.random.key(seed), 5)
    return {
        "density": draw_density(jax.random.fold_in(arg_keys[4], 71), 0),
        "pattern": draw_pattern(jax.random.fold_in(arg_keys[4], 71), 0),
        "square_filter": draw_square_filter(jax.random.fold_in(arg_keys[4], 71), 0),
        "cube_filter": draw_cube_filter(jax.random.fold_in(arg_keys[4], 71), 0),
    }


def matched_slots(listed, targets):
    match = listed[:, None, :] == targets[None, :, None]
    slot_ids = jnp.arange(listed.shape[1], dtype=jnp.int32)
    picked_slot = jnp.sum(jnp.where(match, slot_ids[None, None, :], 0), axis=2).astype(jnp.int32)
    return picked_slot, jnp.any(match, axis=2)


def product_row(row, left_blocks, right_blocks, right_lists, pattern, targets):
    listed = pattern[row]
    source = jnp.where(listed >= 0, listed, row).astype(jnp.int32)
    right_listed = right_lists[source]
    picked_slot, found = matched_slots(right_listed, targets)
    picked = right_blocks[source[:, None], picked_slot]
    picked = jnp.where(found[:, :, None, None], picked, jnp.zeros((), picked.dtype))
    left = left_blocks[row].astype(jnp.float32)
    return jnp.einsum("axy,ajyz->jxz", left, picked.astype(jnp.float32))


def reference(density, pattern, square_filter, cube_filter):
    rows = jnp.arange(NB, dtype=jnp.int32)

    def square_row(row):
        return product_row(row, density, density, pattern, pattern, square_filter[row]).astype(jnp.bfloat16)

    square = lax.map(square_row, rows)

    def purified_row(row):
        targets = cube_filter[row]
        cube = product_row(row, density, square, square_filter, pattern, targets)
        chooser = (targets[:, None] == square_filter[row][None, :]).astype(jnp.float32)
        own_square = jnp.einsum("tj,jxz->txz", chooser, square[row].astype(jnp.float32))
        return 3.0 * own_square - 2.0 * cube

    return lax.map(purified_row, rows)
```

```python
import functools

import jax
import jax.numpy as jnp
from jax import lax
from jax.experimental import pallas as pl
from jax.experimental.pallas import tpu as pltpu
from jax.sharding import PartitionSpec as P

RADIUS = 5
BAND = 2 * RADIUS + 1
ROWS = 8
NEAR = ROWS + 2 * RADIUS
STRIPS = ROWS + 4 * RADIUS
REACH = ROWS + 6 * RADIUS
NT = (((1,), (1,)), ((), ()))
VMEM = pl.BlockSpec(memory_space=pltpu.VMEM)
SMEM = pl.BlockSpec(memory_space=pltpu.SMEM)


def forward_count(j):
    return min(BAND, j + 2 * RADIUS - ROWS + 1)


def forward_list():
    return [(j, o) for j in range(ROWS) for o in range(BAND) if j + o >= ROWS]


def backward_list():
    return [(j, o) for j in range(ROWS) for o in range(BAND) if j + o < BAND - 1]


def forward2_list():
    return [(j, o) for j in range(ROWS) for o in range(BAND) if j + o >= 2 * ROWS]


def backward2_list():
    return [(j, o) for j in range(ROWS) for o in range(BAND) if j + o < BAND - 1 - ROWS]


LISTS = (forward_list(), backward_list(), forward2_list(), backward2_list())
SHIFTS = (1, -1, 2, -2)


def reorder_kernel(off, density, *refs):
    outs, band = refs[:4], refs[4]
    band[...] = jnp.zeros_like(band)
    for i in range(ROWS):
        for s in range(density.shape[1]):
            band[i, off[i, s]] = density[i, s]
    for out, entries in zip(outs, LISTS):
        for e, (j, o) in enumerate(entries):
            out[e] = band[j, o]


def square_kernel(meta, off, sq, l0, l1, l2, l3, h0, h1, h2, h3, square, left, strips):
    col = meta[0]
    strips[...] = jnp.zeros_like(strips)
    left[...] = jnp.zeros_like(left)
    for halo, entries, shift in zip((h0, h1, h2, h3), LISTS, SHIFTS):
        for e, (j, o) in enumerate(entries):
            row = j - shift * ROWS
            strips[row + 2 * RADIUS, row + o] = halo[e]
    for i in range(ROWS):
        for s in range(l0.shape[1]):
            o = off[i, s]
            for b, l in enumerate((l0, l1, l2, l3)):
                start = pl.multiple_of((col ^ b) * 32, 32)
                left[i, o, pl.ds(start, 32), :] = l[i, s]
            used = o < BAND
            strips[jnp.where(used, i + 2 * RADIUS, STRIPS), jnp.where(used, i + o, 0)] = l0[i, s]

    @pl.loop(0, ROWS)
    def _(i):
        w = jnp.concatenate([left[i, o] for o in range(BAND)], axis=1)
        rows = []
        for s in range(square.shape[1]):
            t = sq[i + RADIUS, s] - RADIUS
            rows.append(jnp.concatenate([strips[t, i + o] for o in range(BAND)], axis=1))
        x = jnp.concatenate(rows, axis=0)
        acc = lax.dot_general(x, w, NT, preferred_element_type=jnp.float32)
        square[i] = acc.reshape(square.shape[1:]).astype(square.dtype)


def cube_kernel(meta, sq, cube, before, own, after, left, o0, o1, o2, o3, strips):
    col = meta[0]
    strips[...] = jnp.zeros_like(strips)
    for ref, first in ((before, 0), (own, RADIUS), (after, RADIUS + ROWS)):
        for k in range(ref.shape[0]):
            for s in range(ref.shape[1]):
                strips[sq[first + k, s], first + k] = ref[k, s]
    outs = (o0, o1, o2, o3)
    share = o0.shape[1]

    @pl.loop(0, ROWS)
    def _(i):
        w = jnp.concatenate([left[i, o] for o in range(BAND)], axis=1)
        targets = [cube[i, (col ^ b) * share + q] for b in range(4) for q in range(share)]
        rows = [jnp.concatenate([strips[t, i + o] for o in range(BAND)], axis=1) for t in targets]
        x = jnp.concatenate(rows, axis=0)
        acc = lax.dot_general(x, w, NT, preferred_element_type=jnp.float32)
        for e, t in enumerate(targets):
            mine = strips[t, i + RADIUS].astype(jnp.float32)
            piece = 3.0 * mine - 2.0 * acc[e * 32 : (e + 1) * 32]
            outs[e // share][i, e % share] = piece.astype(o0.dtype)


def final_kernel(meta, p0, p1, p2, p3, out, whole):
    col = meta[0]
    rows = lax.broadcasted_iota(jnp.int32, (128, 128), 0)
    cols = lax.broadcasted_iota(jnp.int32, (128, 128), 1)
    eye = (rows == cols).astype(p0.dtype)
    for b, p in enumerate((p0, p1, p2, p3)):
        start = pl.multiple_of((col ^ b) * 32, 32)
        whole[:, :, pl.ds(start, 32), :] = p[...]

    @pl.loop(0, ROWS)
    def _(i):
        for q in range(out.shape[1]):
            out[i, q] = lax.dot_general(eye, whole[i, q], NT, preferred_element_type=jnp.float32)


def call(kernel, n_smem, outs, scratch, args, flops, limit=40):
    size = sum(a.size * a.dtype.itemsize for a in args[n_smem:])
    size += sum(o.size * o.dtype.itemsize for o in outs)
    return pl.pallas_call(
        kernel,
        out_shape=outs,
        in_specs=[SMEM] * n_smem + [VMEM] * (len(args) - n_smem),
        out_specs=[VMEM] * len(outs),
        scratch_shapes=scratch,
        compiler_params=pltpu.CompilerParams(vmem_limit_bytes=limit << 20),
        cost_estimate=pl.CostEstimate(flops=flops, bytes_accessed=size, transcendentals=0),
    )(*args)


def shape(*dims, dtype=jnp.bfloat16):
    return jax.ShapeDtypeStruct(dims, dtype)


def per_device(density, pattern, square_filter, cube_filter):
    layers = lax.axis_size("layer")
    groups = lax.axis_size("row") * layers
    total = groups * ROWS
    assert density.shape[0] == ROWS and lax.axis_size("col") == 4
    piece = density.shape[2:]
    col = lax.axis_index("col")
    first = (lax.axis_index("row") * layers + lax.axis_index("layer")) * ROWS

    def shifted(x, d):
        return lax.ppermute(x, ("row", "layer"), [(g, (g + d) % groups) for g in range(groups)])

    def across(x, bits):
        return lax.ppermute(x, "col", [(c, c ^ bits) for c in range(4)])

    meta = jnp.reshape(col, (1,)).astype(jnp.int32)
    own_rows = first + jnp.arange(ROWS, dtype=jnp.int32)[:, None]
    listed = lax.dynamic_slice_in_dim(pattern, first, ROWS, 0)
    off = jnp.where(listed >= 0, (listed - own_rows + RADIUS + total) % total, BAND)
    near = (first - RADIUS + jnp.arange(NEAR, dtype=jnp.int32) + total) % total
    low = first - 3 * RADIUS
    sq = (jnp.take(square_filter, near, axis=0) - low + total) % total
    cube = (lax.dynamic_slice_in_dim(cube_filter, first, ROWS, 0) - low + total) % total

    l2 = across(density, 2)
    l1 = across(density, 1)
    payload = call(
        reorder_kernel, 1, [shape(len(e), *piece) for e in LISTS],
        [pltpu.VMEM((ROWS, BAND + 1, *piece), density.dtype)], (off, density), 0,
    )
    halos = [shifted(p, d) for p, d in zip(payload, SHIFTS)]
    l3 = across(l2, 1)

    kept = square_filter.shape[1]
    square, left = call(
        square_kernel, 3,
        [shape(ROWS, kept, *piece), shape(ROWS, BAND + 1, 128, 128)],
        [pltpu.VMEM((STRIPS + 1, NEAR, *piece), density.dtype)],
        (meta, off, sq, density, l1, l2, l3, *halos), 2 * ROWS * kept * BAND * 128 * 128 * 32,
    )
    before = shifted(square[ROWS - RADIUS :], 1)
    after = shifted(square[:RADIUS], -1)
    slots = cube_filter.shape[1]
    share = slots // 4
    pieces = call(
        cube_kernel, 3, [shape(ROWS, share, *piece)] * 4,
        [pltpu.VMEM((REACH, NEAR, *piece), density.dtype)],
        (meta, sq, cube, before, square, after, left), 2 * ROWS * slots * BAND * 128 * 128 * 32,
    )
    got = [pieces[0]] + [across(pieces[b], b) for b in (1, 2, 3)]
    return call(
        final_kernel, 1, [shape(ROWS, share, 128, 128, dtype=jnp.float32)],
        [pltpu.VMEM((ROWS, share, 128, 128), density.dtype)], (meta, *got), 2 * ROWS * share * 128**3,
    )[0]


def solution(mesh):
    in_specs = (P(("row", "layer"), None, "col", None), P(), P(), P())
    out_specs = P(("row", "layer"), "col", None, None)
    return jax.shard_map(
        per_device, mesh=mesh, in_specs=in_specs, out_specs=out_specs, check_vma=False
    )
```

```python
import functools

import jax
import jax.numpy as jnp
from jax import lax
from jax.experimental import pallas as pl
from jax.experimental.pallas import tpu as pltpu
from jax.sharding import PartitionSpec as P

RADIUS = 5
BAND = 2 * RADIUS + 1
ROWS = 8
NEAR = ROWS + 2 * RADIUS
STRIPS = ROWS + 4 * RADIUS
REACH = ROWS + 6 * RADIUS
NT = (((1,), (1,)), ((), ()))
VMEM = pl.BlockSpec(memory_space=pltpu.VMEM)
SMEM = pl.BlockSpec(memory_space=pltpu.SMEM)


def forward_count(j):
    return min(BAND, j + 2 * RADIUS - ROWS + 1)


def forward_list():
    return [(j, o) for j in range(ROWS) for o in range(BAND) if j + o >= ROWS]


def backward_list():
    return [(j, o) for j in range(ROWS) for o in range(BAND) if j + o < BAND - 1]


def forward2_list():
    return [(j, o) for j in range(ROWS) for o in range(BAND) if j + o >= 2 * ROWS]


def backward2_list():
    return [(j, o) for j in range(ROWS) for o in range(BAND) if j + o < BAND - 1 - ROWS]


LISTS = (forward_list(), backward_list(), forward2_list(), backward2_list())
SHIFTS = (1, -1, 2, -2)


def reorder_kernel(meta, pattern, density, *refs):
    outs, band = refs[:4], refs[4]
    first, total = meta[1], pattern.shape[0]
    band[...] = jnp.zeros_like(band)
    for i in range(ROWS):
        for s in range(density.shape[1]):
            listed = pattern[first + i, s]
            o = listed - (first + i) + RADIUS
            o = jnp.where(o < 0, o + total, jnp.where(o >= total, o - total, o))
            band[i, jnp.where(listed >= 0, o, BAND)] = density[i, s]
    for out, entries in zip(outs, LISTS):
        for e, (j, o) in enumerate(entries):
            out[e] = band[j, o]


def square_kernel(meta, off, sq, l0, l1, l2, l3, h0, h1, h2, h3, square, left, strips):
    col = meta[0]
    strips[...] = jnp.zeros_like(strips)
    left[...] = jnp.zeros_like(left)
    for halo, entries, shift in zip((h0, h1, h2, h3), LISTS, SHIFTS):
        for e, (j, o) in enumerate(entries):
            row = j - shift * ROWS
            strips[row + 2 * RADIUS, row + o] = halo[e]
    for i in range(ROWS):
        for s in range(l0.shape[1]):
            o = off[i, s]
            for b, l in enumerate((l0, l1, l2, l3)):
                start = pl.multiple_of((col ^ b) * 32, 32)
                left[i, o, pl.ds(start, 32), :] = l[i, s]
            used = o < BAND
            strips[jnp.where(used, i + 2 * RADIUS, STRIPS), jnp.where(used, i + o, 0)] = l0[i, s]

    @pl.loop(0, ROWS)
    def _(i):
        w = jnp.concatenate([left[i, o] for o in range(BAND)], axis=1)
        rows = []
        for s in range(square.shape[1]):
            t = sq[i + RADIUS, s] - RADIUS
            rows.append(jnp.concatenate([strips[t, i + o] for o in range(BAND)], axis=1))
        x = jnp.concatenate(rows, axis=0)
        acc = lax.dot_general(x, w, NT, preferred_element_type=jnp.float32)
        square[i] = acc.reshape(square.shape[1:]).astype(square.dtype)


def cube_kernel(meta, sq, cube, before, own, after, left, o0, o1, o2, o3, strips):
    col = meta[0]
    strips[...] = jnp.zeros_like(strips)
    for ref, first in ((before, 0), (own, RADIUS), (after, RADIUS + ROWS)):
        for k in range(ref.shape[0]):
            for s in range(ref.shape[1]):
                strips[sq[first + k, s], first + k] = ref[k, s]
    outs = (o0, o1, o2, o3)
    share = o0.shape[1]

    @pl.loop(0, ROWS)
    def _(i):
        w = jnp.concatenate([left[i, o] for o in range(BAND)], axis=1)
        targets = [cube[i, (col ^ b) * share + q] for b in range(4) for q in range(share)]
        rows = [jnp.concatenate([strips[t, i + o] for o in range(BAND)], axis=1) for t in targets]
        x = jnp.concatenate(rows, axis=0)
        acc = lax.dot_general(x, w, NT, preferred_element_type=jnp.float32)
        for e, t in enumerate(targets):
            mine = strips[t, i + RADIUS].astype(jnp.float32)
            piece = 3.0 * mine - 2.0 * acc[e * 32 : (e + 1) * 32]
            outs[e // share][i, e % share] = piece.astype(o0.dtype)


def final_kernel(meta, p0, p1, p2, p3, out, whole):
    col = meta[0]
    rows = lax.broadcasted_iota(jnp.int32, (128, 128), 0)
    cols = lax.broadcasted_iota(jnp.int32, (128, 128), 1)
    eye = (rows == cols).astype(p0.dtype)
    for b, p in enumerate((p0, p1, p2, p3)):
        start = pl.multiple_of((col ^ b) * 32, 32)
        whole[:, :, pl.ds(start, 32), :] = p[...]

    @pl.loop(0, ROWS)
    def _(i):
        for q in range(out.shape[1]):
            out[i, q] = lax.dot_general(eye, whole[i, q], NT, preferred_element_type=jnp.float32)


def call(kernel, n_smem, outs, scratch, args, flops, limit=16):
    size = sum(a.size * a.dtype.itemsize for a in args[n_smem:])
    size += sum(o.size * o.dtype.itemsize for o in outs)
    return pl.pallas_call(
        kernel,
        out_shape=outs,
        in_specs=[SMEM] * n_smem + [VMEM] * (len(args) - n_smem),
        out_specs=[VMEM] * len(outs),
        scratch_shapes=scratch,
        compiler_params=pltpu.CompilerParams(vmem_limit_bytes=limit << 20),
        cost_estimate=pl.CostEstimate(flops=flops, bytes_accessed=size, transcendentals=0),
    )(*args)


def shape(*dims, dtype=jnp.bfloat16):
    return jax.ShapeDtypeStruct(dims, dtype)


def per_device(density, pattern, square_filter, cube_filter):
    layers = lax.axis_size("layer")
    groups = lax.axis_size("row") * layers
    total = groups * ROWS
    assert density.shape[0] == ROWS and lax.axis_size("col") == 4
    piece = density.shape[2:]
    col = lax.axis_index("col")
    first = (lax.axis_index("row") * layers + lax.axis_index("layer")) * ROWS

    def shifted(x, d):
        return lax.ppermute(x, ("row", "layer"), [(g, (g + d) % groups) for g in range(groups)])

    def across(x, bits):
        return lax.ppermute(x, "col", [(c, c ^ bits) for c in range(4)])

    meta = jnp.stack([col, first]).astype(jnp.int32)
    own_rows = first + jnp.arange(ROWS, dtype=jnp.int32)[:, None]
    listed = lax.dynamic_slice_in_dim(pattern, first, ROWS, 0)
    off = jnp.where(listed >= 0, (listed - own_rows + RADIUS + total) % total, BAND)
    near = (first - RADIUS + jnp.arange(NEAR, dtype=jnp.int32) + total) % total
    low = first - 3 * RADIUS
    sq = (jnp.take(square_filter, near, axis=0) - low + total) % total
    cube = (lax.dynamic_slice_in_dim(cube_filter, first, ROWS, 0) - low + total) % total

    l2 = across(density, 2)
    l1 = across(density, 1)
    payload = call(
        reorder_kernel, 2, [shape(len(e), *piece) for e in LISTS],
        [pltpu.VMEM((ROWS, BAND + 1, *piece), density.dtype)], (meta, pattern, density), 0,
    )
    payload, l1 = lax.optimization_barrier((payload, l1))
    halos = [shifted(p, d) for p, d in zip(payload, SHIFTS)]
    l2, halos = lax.optimization_barrier((l2, halos))
    l3 = across(l2, 1)

    kept = square_filter.shape[1]
    square, left = call(
        square_kernel, 3,
        [shape(ROWS, kept, *piece), shape(ROWS, BAND + 1, 128, 128)],
        [pltpu.VMEM((STRIPS + 1, NEAR, *piece), density.dtype)],
        (meta, off, sq, density, l1, l2, l3, *halos), 2 * ROWS * kept * BAND * 128 * 128 * 32,
    )
    before = shifted(square[ROWS - RADIUS :], 1)
    after = shifted(square[:RADIUS], -1)
    slots = cube_filter.shape[1]
    share = slots // 4
    pieces = call(
        cube_kernel, 3, [shape(ROWS, share, *piece)] * 4,
        [pltpu.VMEM((REACH, NEAR, *piece), density.dtype)],
        (meta, sq, cube, before, square, after, left), 2 * ROWS * slots * BAND * 128 * 128 * 32,
    )
    got = [pieces[0]] + [across(pieces[b], b) for b in (1, 2, 3)]
    return call(
        final_kernel, 1, [shape(ROWS, share, 128, 128, dtype=jnp.float32)],
        [pltpu.VMEM((ROWS, share, 128, 128), density.dtype)], (meta, *got), 2 * ROWS * share * 128**3,
    )[0]


def solution(mesh):
    in_specs = (P(("row", "layer"), None, "col", None), P(), P(), P())
    out_specs = P(("row", "layer"), "col", None, None)
    return jax.shard_map(
        per_device, mesh=mesh, in_specs=in_specs, out_specs=out_specs, check_vma=False
    )
```

```python
import jax
import jax.numpy as jnp
from jax import lax
from jax.experimental import pallas as pl
from jax.experimental.pallas import tpu as pltpu
from jax.sharding import PartitionSpec as P

RADIUS = 5
BAND = 2 * RADIUS + 1
ROWS = 8
NEAR = ROWS + 2 * RADIUS
STRIPS = ROWS + 4 * RADIUS
REACH = ROWS + 6 * RADIUS
NT = (((1,), (1,)), ((), ()))
VMEM = pl.BlockSpec(memory_space=pltpu.VMEM)
SMEM = pl.BlockSpec(memory_space=pltpu.SMEM)

SHIFTS = (1, -1, 2, -2)
OWN = [(j, o) for j in range(ROWS) for o in range(BAND)]
LISTS = (
    [(j, o) for j, o in OWN if ROWS <= j + o <= ROWS + RADIUS - 1],
    [(j, o) for j, o in OWN if RADIUS <= j + o <= 2 * RADIUS - 1],
    [(j, o) for j, o in OWN if j + o >= 2 * ROWS],
    [(j, o) for j, o in OWN if j + o < BAND - 1 - ROWS],
)
EDGE = [(m, o) for m, o in OWN if not RADIUS <= m + o < RADIUS + ROWS]


def wrapped(value, total):
    return jnp.where(value < 0, value + total, jnp.where(value >= total, value - total, value))


def offset_slot(pattern, i, s, first):
    listed = pattern[s, first + i]
    o = wrapped(listed - (first + i) + RADIUS, pattern.shape[1])
    return jnp.where(listed >= 0, o, BAND)


def reorder_kernel(meta, pattern, density, *refs):
    outs, band = refs[:4], refs[4]
    first = meta[1]
    band[...] = jnp.zeros_like(band)
    for i in range(ROWS):
        for s in range(density.shape[1]):
            band[i, offset_slot(pattern, i, s, first)] = density[i, s]
    for out, entries in zip(outs, LISTS):
        for e, (j, o) in enumerate(entries):
            out[e] = band[j, o]


def place(left, piece, i, o, s, col, b):
    left[i, o, pl.ds(pl.multiple_of((col ^ b) * 32, 32), 32), :] = piece[i, s]


def prepare_kernel(meta, pattern, l0, l1, strips, left):
    col, first = meta[0], meta[1]
    strips[...] = jnp.zeros_like(strips)
    left[...] = jnp.zeros_like(left)
    for i in range(ROWS):
        for s in range(l0.shape[1]):
            o = offset_slot(pattern, i, s, first)
            place(left, l0, i, o, s, col, 0)
            place(left, l1, i, o, s, col, 1)
            used = o < BAND
            strips[jnp.where(used, i + 2 * RADIUS, STRIPS), jnp.where(used, i + o, 0)] = l0[i, s]


def square_kernel(meta, pattern, kept, l2, l3, h0, h1, h2, h3, strips_in, left_in,
                  square, low, high, strips, left):
    del strips_in, left_in
    col, first = meta[0], meta[1]
    for halo, entries, shift in zip((h0, h1, h2, h3), LISTS, SHIFTS):
        for e, (j, o) in enumerate(entries):
            row = j - shift * ROWS
            strips[row + 2 * RADIUS, row + o] = halo[e]
    for i in range(ROWS):
        for s in range(l2.shape[1]):
            o = offset_slot(pattern, i, s, first)
            place(left, l2, i, o, s, col, 2)
            place(left, l3, i, o, s, col, 3)
    shape = (32, 128)
    pick = lax.broadcasted_iota(jnp.int32, shape, 1) == lax.broadcasted_iota(jnp.int32, shape, 0) + col * 32
    pick = pick.astype(left.dtype)
    for m, o in EDGE:
        turned = lax.dot_general(pick, left[m, o], NT, preferred_element_type=jnp.float32)
        strips[m + o + RADIUS, m + RADIUS] = turned.astype(strips.dtype)

    @pl.loop(0, ROWS)
    def _(i):
        w = jnp.concatenate([left[i, o] for o in range(BAND)], axis=1)
        rows = []
        for s in range(square.shape[1]):
            t = wrapped(kept[s, first + i] - first + 2 * RADIUS, kept.shape[1])
            rows.append(jnp.concatenate([strips[t, i + o] for o in range(BAND)], axis=1))
        x = jnp.concatenate(rows, axis=0)
        acc = lax.dot_general(x, w, NT, preferred_element_type=jnp.float32)
        square[i] = acc.reshape(square.shape[1:]).astype(square.dtype)

    low[...] = square[:RADIUS]
    high[...] = square[ROWS - RADIUS :]


def gather_dot(strips, left, targets, i, offsets):
    w = jnp.concatenate([left[i, o] for o in offsets], axis=1)
    rows = [jnp.concatenate([strips[t, i + o] for o in offsets], axis=1) for t in targets]
    x = jnp.concatenate(rows, axis=0)
    return lax.dot_general(x, w, NT, preferred_element_type=jnp.float32)


def strip_of(table, s, row, first):
    total = table.shape[1]
    return wrapped(table[s, wrapped(row, total)] - first + 3 * RADIUS, total)


def cube_targets(cube, i, col, first, share):
    return [strip_of(cube, (col ^ b) * share + q, first + i, first) for b in range(4) for q in range(share)]


def inner_kernel(meta, kept, cube, own, left, strips, partial):
    col, first = meta[0], meta[1]
    strips[...] = jnp.zeros_like(strips)
    for k in range(ROWS):
        for s in range(own.shape[1]):
            strips[strip_of(kept, s, first + k, first), RADIUS + k] = own[k, s]
    share = cube.shape[0] // 4
    for i in range(ROWS):
        targets = cube_targets(cube, i, col, first, share)
        offsets = [o for o in range(BAND) if RADIUS <= i + o < RADIUS + ROWS]
        acc = gather_dot(strips, left, targets, i, offsets)
        for e, t in enumerate(targets):
            mine = strips[t, i + RADIUS].astype(jnp.float32)
            partial[i, e] = 3.0 * mine - 2.0 * acc[e * 32 : (e + 1) * 32]


def cube_kernel(meta, kept, cube, before, after, left, partial, strips_in, o0, o1, o2, o3, strips):
    del strips_in
    col, first = meta[0], meta[1]
    for k in range(RADIUS):
        for s in range(before.shape[1]):
            strips[strip_of(kept, s, first - RADIUS + k, first), k] = before[k, s]
            strips[strip_of(kept, s, first + ROWS + k, first), RADIUS + ROWS + k] = after[k, s]
    outs = (o0, o1, o2, o3)
    share = o0.shape[1]
    for i in range(ROWS):
        targets = cube_targets(cube, i, col, first, share)
        offsets = [o for o in range(BAND) if not RADIUS <= i + o < RADIUS + ROWS]
        acc = gather_dot(strips, left, targets, i, offsets)
        for e in range(len(targets)):
            piece = partial[i, e] - 2.0 * acc[e * 32 : (e + 1) * 32]
            outs[e // share][i, e % share] = piece.astype(o0.dtype)


def final_kernel(meta, p0, p1, p2, p3, out, whole):
    col = meta[0]
    rows = lax.broadcasted_iota(jnp.int32, (128, 128), 0)
    cols = lax.broadcasted_iota(jnp.int32, (128, 128), 1)
    eye = (rows == cols).astype(p0.dtype)
    for b, p in enumerate((p0, p1, p2, p3)):
        start = pl.multiple_of((col ^ b) * 32, 32)
        whole[:, pl.ds(start, 32), :] = p[0]
    for q in range(out.shape[1]):
        out[0, q] = lax.dot_general(eye, whole[q], NT, preferred_element_type=jnp.float32)


def call(kernel, specs, outs, scratch, args, flops=0, limit=16, aliases=None):
    size = sum(a.size * a.dtype.itemsize for a in args) + sum(o.size * o.dtype.itemsize for o in outs)
    return pl.pallas_call(
        kernel,
        out_shape=outs,
        in_specs=specs,
        out_specs=[VMEM] * len(outs),
        scratch_shapes=scratch,
        input_output_aliases=aliases or {},
        compiler_params=pltpu.CompilerParams(vmem_limit_bytes=limit << 20),
        cost_estimate=pl.CostEstimate(flops=flops, bytes_accessed=size, transcendentals=0),
    )(*args)


def shape(*dims, dtype=jnp.bfloat16):
    return jax.ShapeDtypeStruct(dims, dtype)


def per_device(density, pattern, square_filter, cube_filter):
    layers = lax.axis_size("layer")
    groups = lax.axis_size("row") * layers
    assert density.shape[0] == ROWS and lax.axis_size("col") == 4
    piece = density.shape[2:]
    col = lax.axis_index("col")
    first = (lax.axis_index("row") * layers + lax.axis_index("layer")) * ROWS
    meta = jnp.stack([col, first]).astype(jnp.int32)
    pattern, kept, cube = pattern.T, square_filter.T, cube_filter.T

    def shifted(x, d):
        return lax.ppermute(x, ("row", "layer"), [(g, (g + d) % groups) for g in range(groups)])

    def across(x, bits):
        return lax.ppermute(x, "col", [(c, c ^ bits) for c in range(4)])

    l2 = across(density, 2)
    l1 = across(density, 1)
    payload = call(
        reorder_kernel, [SMEM, SMEM, VMEM], [shape(len(e), *piece) for e in LISTS],
        [pltpu.VMEM((ROWS, BAND + 1, *piece), density.dtype)],
        (meta, pattern, density),
    )
    payload, l1 = lax.optimization_barrier((payload, l1))
    halos = [shifted(p, d) for p, d in zip(payload, SHIFTS)]
    strips, left = call(
        prepare_kernel, [SMEM, SMEM, VMEM, VMEM],
        [shape(STRIPS + 1, NEAR, *piece), shape(ROWS, BAND + 1, 128, 128)],
        [], (meta, pattern, density, l1),
    )
    l2, halos, strips, left = lax.optimization_barrier((l2, halos, strips, left))
    l3 = across(l2, 1)

    width = kept.shape[0]
    square, low, high, _, left = call(
        square_kernel, [SMEM] * 3 + [VMEM] * 8,
        [shape(ROWS, width, *piece), shape(RADIUS, width, *piece), shape(RADIUS, width, *piece),
         shape(*strips.shape), shape(*left.shape)],
        [], (meta, pattern, kept, l2, l3, *halos, strips, left),
        2 * ROWS * width * BAND * 128 * 128 * 32, aliases={9: 3, 10: 4},
    )
    after = shifted(low, -1)
    before = shifted(high, 1)
    slots = cube.shape[0]
    share = slots // 4
    work = 2 * ROWS * slots * BAND * 128 * 128 * 32
    strips, partial = call(
        inner_kernel, [SMEM] * 3 + [VMEM] * 2,
        [shape(REACH, NEAR, *piece), shape(ROWS, slots, *piece, dtype=jnp.float32)],
        [], (meta, kept, cube, square, left), work * 2 // 3,
    )
    pieces = call(
        cube_kernel, [SMEM] * 3 + [VMEM] * 5,
        [shape(ROWS, share, *piece)] * 4 + [shape(*strips.shape)],
        [], (meta, kept, cube, before, after, left, partial, strips), work // 3,
        aliases={7: 4},
    )
    got = [pieces[0]] + [across(pieces[b], b) for b in (1, 2, 3)]
    return pl.pallas_call(
        final_kernel,
        grid=(ROWS,),
        out_shape=shape(ROWS, share, 128, 128, dtype=jnp.float32),
        in_specs=[SMEM] + [pl.BlockSpec((1, share, *piece), lambda i: (i, 0, 0, 0))] * 4,
        out_specs=pl.BlockSpec((1, share, 128, 128), lambda i: (i, 0, 0, 0)),
        scratch_shapes=[pltpu.VMEM((share, 128, 128), density.dtype)],
        compiler_params=pltpu.CompilerParams(vmem_limit_bytes=16 << 20),
    )(meta, *got)


def solution(mesh):
    in_specs = (P(("row", "layer"), None, "col", None), P(), P(), P())
    out_specs = P(("row", "layer"), "col", None, None)
    return jax.shard_map(
        per_device, mesh=mesh, in_specs=in_specs, out_specs=out_specs, check_vma=False
    )
```

```python
import jax
import jax.numpy as jnp
from jax import lax
from jax.experimental import pallas as pl
from jax.experimental.pallas import tpu as pltpu
from jax.sharding import PartitionSpec as P

RADIUS = 5
BAND = 2 * RADIUS + 1
ROWS = 8
NEAR = ROWS + 2 * RADIUS
STRIPS = ROWS + 4 * RADIUS
REACH = ROWS + 6 * RADIUS
NT = (((1,), (1,)), ((), ()))
VMEM = pl.BlockSpec(memory_space=pltpu.VMEM)
SMEM = pl.BlockSpec(memory_space=pltpu.SMEM)
ANY = pl.BlockSpec(memory_space=pl.ANY)

SHIFTS = (1, -1, 2, -2)
OWN = [(j, o) for j in range(ROWS) for o in range(BAND)]
LISTS = (
    [(j, o) for j, o in OWN if ROWS <= j + o <= ROWS + RADIUS - 1],
    [(j, o) for j, o in OWN if RADIUS <= j + o <= 2 * RADIUS - 1],
    [(j, o) for j, o in OWN if j + o >= 2 * ROWS],
    [(j, o) for j, o in OWN if j + o < BAND - 1 - ROWS],
)
EDGES = (
    [(m, o) for m, o in OWN if m + o < RADIUS],
    [(m, o) for m, o in OWN if m + o >= RADIUS + ROWS],
)
LATE = range(RADIUS, ROWS)
MIDDLE = range(ROWS - RADIUS, RADIUS)
EARLY = range(0, ROWS - RADIUS)
AFTER = range(RADIUS + ROWS, NEAR)
CLOSE = range(ROWS - RADIUS, RADIUS)
FAR = range(0, ROWS - RADIUS)


def wrapped(value, total):
    return jnp.where(value < 0, value + total, jnp.where(value >= total, value - total, value))


def offset_slot(pattern, i, s, first):
    listed = pattern[s, first + i]
    o = wrapped(listed - (first + i) + RADIUS, pattern.shape[1])
    return jnp.where(listed >= 0, o, BAND)


def position(pattern, i, s, first):
    o = offset_slot(pattern, i, s, first)
    return jnp.where(o < BAND, i + o, (i + BAND) % NEAR)


def reorder_kernel(meta, pattern, density, h0, h1, h2, h3, band, blocks, table, sems):
    first = meta[1]
    copies = (
        pltpu.make_async_copy(density, blocks, sems.at[0]),
        pltpu.make_async_copy(pattern, table, sems.at[1]),
    )
    for copy in copies:
        copy.start()
    band[...] = jnp.zeros_like(band)
    for copy in copies:
        copy.wait()
    for i in range(ROWS):
        for s in range(blocks.shape[1]):
            band[i, offset_slot(table, i, s, first)] = blocks[i, s]
    for out, entries in zip((h0, h1, h2, h3), LISTS):
        for e, (j, o) in enumerate(entries):
            out[e] = band[j, o]


def place(left, piece, i, p, s, col, b):
    left[i, p, pl.ds(pl.multiple_of((col ^ b) * 32, 32), 32), :] = piece[i, s]


def prepare_kernel(meta, pattern, l0, l1, strips, left):
    col, first = meta[0], meta[1]
    strips[...] = jnp.zeros_like(strips)
    left[...] = jnp.zeros_like(left)
    for i in range(ROWS):
        for s in range(l0.shape[1]):
            p = position(pattern, i, s, first)
            place(left, l0, i, p, s, col, 0)
            place(left, l1, i, p, s, col, 1)
            strips[i + 2 * RADIUS, p] = l0[i, s]


def insert_kernel(meta, pattern, l2, h0, h1, h2, h3, strips_in, left_in, strips, left):
    del strips_in, left_in
    col, first = meta[0], meta[1]
    for halo, entries, shift in zip((h0, h1, h2, h3), LISTS, SHIFTS):
        for e, (j, o) in enumerate(entries):
            row = j - shift * ROWS
            strips[row + 2 * RADIUS, row + o] = halo[e]
    for i in range(ROWS):
        for s in range(l2.shape[1]):
            place(left, l2, i, position(pattern, i, s, first), s, col, 2)


def gather_dot(strips, left, targets, i, places):
    w = jnp.concatenate([left[i, p] for p in places], axis=1)
    rows = [jnp.concatenate([strips[t, p] for p in places], axis=1) for t in targets]
    x = jnp.concatenate(rows, axis=0)
    return lax.dot_general(x, w, NT, preferred_element_type=jnp.float32)


def square_row(kept, strips, left, i, first):
    total = kept.shape[1]
    targets = [wrapped(kept[s, first + i] - first + 2 * RADIUS, total) for s in range(kept.shape[0])]
    acc = gather_dot(strips, left, targets, i, range(i, i + BAND))
    return acc.reshape(len(targets), 32, 128).astype(strips.dtype)


def low_kernel(meta, pattern, kept, l3, strips_in, left_in, low, strips, left):
    del strips_in, left_in
    col, first = meta[0], meta[1]
    for i in range(ROWS):
        for s in range(l3.shape[1]):
            place(left, l3, i, position(pattern, i, s, first), s, col, 3)
    shape = (32, 128)
    pick = lax.broadcasted_iota(jnp.int32, shape, 1) == lax.broadcasted_iota(jnp.int32, shape, 0) + col * 32
    pick = pick.astype(left.dtype)
    for edge in EDGES:
        blocks = jnp.concatenate([left[m, m + o] for m, o in edge], axis=0)
        turned = lax.dot_general(pick, blocks, NT, preferred_element_type=jnp.float32)
        for e, (m, o) in enumerate(edge):
            strips[m + o + RADIUS, m + RADIUS] = turned[:, e * 128 : (e + 1) * 128].astype(strips.dtype)
    for i in range(RADIUS):
        low[i] = square_row(kept, strips, left, i, first)


def high_kernel(meta, kept, low, strips, left, far, close):
    first = meta[1]
    for i in range(RADIUS, ROWS):
        row = square_row(kept, strips, left, i, first)
        if i < ROWS - len(CLOSE):
            far[i - ROWS + RADIUS] = row
        else:
            close[i - ROWS + len(CLOSE)] = row
    for i in range(ROWS - RADIUS, RADIUS):
        far[i - ROWS + RADIUS] = low[i]


def strip_of(table, s, row, first):
    total = table.shape[1]
    return wrapped(table[s, wrapped(row, total)] - first + 3 * RADIUS, total)


def cube_targets(cube, i, col, first, share):
    return [strip_of(cube, (col ^ b) * share + q, first + i, first) for b in range(4) for q in range(share)]


def insert_rows(strips, kept, rows, places, first):
    for k, p in enumerate(places):
        for s in range(rows.shape[1]):
            strips[strip_of(kept, s, first - RADIUS + p, first), p] = rows[k, s]


def inner_kernel(meta, kept, cube, low, far, close, left, strips, partial):
    col, first = meta[0], meta[1]
    strips[...] = jnp.zeros_like(strips)
    insert_rows(strips, kept, low, range(RADIUS, 2 * RADIUS), first)
    insert_rows(strips, kept, far, range(ROWS, ROWS + len(FAR)), first)
    insert_rows(strips, kept, close, range(RADIUS + ROWS - len(CLOSE), RADIUS + ROWS), first)
    share = cube.shape[0] // 4

    @pl.loop(0, ROWS)
    def _(i):
        targets = cube_targets(cube, i, col, first, share)
        acc = gather_dot(strips, left, targets, i, range(RADIUS, RADIUS + ROWS))
        for e, t in enumerate(targets):
            mine = strips[t, i + RADIUS].astype(jnp.float32)
            partial[i, e] = 3.0 * mine - 2.0 * acc[e * 32 : (e + 1) * 32]


def outer_kernel(rows, places, arrived):
    def kernel(meta, kept, cube, halo, left, partial, strips_in, o0, o1, o2, o3, strips):
        del strips_in
        col, first = meta[0], meta[1]
        insert_rows(strips, kept, halo, arrived, first)
        share = cube.shape[0] // 4
        for n, i in enumerate(rows):
            targets = cube_targets(cube, i, col, first, share)
            acc = gather_dot(strips, left, targets, i, [p for p in places if i <= p < i + BAND])
            for e in range(len(targets)):
                piece = partial[i, e] - 2.0 * acc[e * 32 : (e + 1) * 32]
                (o0, o1, o2, o3)[e // share][n, e % share] = piece.astype(o0.dtype)

    return kernel


def final_kernel(parts, aliased):
    def kernel(meta, *refs):
        col = meta[0]
        out, whole, turned, sems = refs[-4:]
        copies = []
        for n, rows in enumerate(parts):
            for b, p in enumerate(refs[4 * n : 4 * n + 4]):
                start = pl.multiple_of((col ^ b) * 32, 32)
                whole[pl.ds(rows[0], len(rows)), :, pl.ds(start, 32), :] = p[...]
            for i in rows:
                for q in range(out.shape[1]):
                    turned[i, q] = whole[i, q].T.astype(turned.dtype)
                copies.append(pltpu.make_async_copy(turned.at[i], out.at[i], sems.at[i]))
                copies[-1].start()
        for copy in copies:
            copy.wait()

    return kernel


def shape(*dims, dtype=jnp.bfloat16):
    return jax.ShapeDtypeStruct(dims, dtype)


def call(kernel, specs, outs, args, scratch=(), flops=0, aliases=None, out_specs=None, limit=16):
    size = sum(a.size * a.dtype.itemsize for a in args) + sum(o.size * o.dtype.itemsize for o in outs)
    return pl.pallas_call(
        kernel,
        out_shape=outs,
        in_specs=specs,
        out_specs=out_specs or [VMEM] * len(outs),
        scratch_shapes=scratch,
        input_output_aliases=aliases or {},
        compiler_params=pltpu.CompilerParams(vmem_limit_bytes=limit << 20),
        cost_estimate=pl.CostEstimate(flops=flops, bytes_accessed=size, transcendentals=0),
    )(*args)


def per_device(density, pattern, square_filter, cube_filter):
    layers = lax.axis_size("layer")
    groups = lax.axis_size("row") * layers
    assert density.shape[0] == ROWS and lax.axis_size("col") == 4
    piece = density.shape[2:]
    col = lax.axis_index("col")
    first = (lax.axis_index("row") * layers + lax.axis_index("layer")) * ROWS
    meta = jnp.stack([col, first]).astype(jnp.int32)
    pattern, kept, cube = pattern.T, square_filter.T, cube_filter.T
    width, slots = kept.shape[0], cube.shape[0]
    share = slots // 4

    def shifted(x, d):
        return lax.ppermute(x, ("row", "layer"), [(g, (g + d) % groups) for g in range(groups)])

    def across(x, bits):
        return lax.ppermute(x, "col", [(c, c ^ bits) for c in range(4)])

    l2 = across(density, 2)
    l1 = across(density, 1)
    payload = call(
        reorder_kernel, [SMEM, ANY, ANY], [shape(len(e), *piece) for e in LISTS], (meta, pattern, density),
        [pltpu.VMEM((ROWS, BAND + 1, *piece), density.dtype), pltpu.VMEM(density.shape, density.dtype),
         pltpu.SMEM(pattern.shape, pattern.dtype), pltpu.SemaphoreType.DMA((2,))],
    )
    payload, l1 = lax.optimization_barrier((payload, l1))
    halos = [shifted(p, d) for p, d in zip(payload, SHIFTS)]
    strips, left = call(
        prepare_kernel, [SMEM] * 2 + [VMEM] * 2,
        [shape(STRIPS, NEAR, *piece), shape(ROWS, NEAR, 128, 128)], (meta, pattern, density, l1),
    )
    l2, halos, strips, left = lax.optimization_barrier((l2, halos, strips, left))
    l3 = across(l2, 1)
    both = [shape(*strips.shape), shape(*left.shape)]
    strips, left = call(
        insert_kernel, [SMEM] * 2 + [VMEM] * 7, both, (meta, pattern, l2, *halos, strips, left),
        aliases={7: 0, 8: 1},
    )
    work = 2 * width * BAND * 128 * 128 * 32
    low, strips, left = call(
        low_kernel, [SMEM] * 3 + [VMEM] * 3, [shape(RADIUS, width, *piece), *both],
        (meta, pattern, kept, l3, strips, left), flops=work * RADIUS, aliases={4: 1, 5: 2},
    )
    after = shifted(low, -1)
    far, close = call(
        high_kernel, [SMEM] * 2 + [VMEM] * 3,
        [shape(len(FAR), width, *piece), shape(len(CLOSE), width, *piece)],
        (meta, kept, low, strips, left), flops=work * (ROWS - RADIUS),
    )
    close_in = shifted(close, 1)
    far_in = shifted(far, 1)

    tables = (meta, kept, cube)
    strips, partial = call(
        inner_kernel, [SMEM] * 3 + [VMEM] * 4,
        [shape(REACH, NEAR, *piece), shape(ROWS, slots, *piece, dtype=jnp.float32)],
        (*tables, low, far, close, left), flops=2 * slots * ROWS * ROWS * 128 * 128 * 32,
    )
    parts = []
    for rows, places, arrived, halo in (
        (LATE, AFTER, AFTER, after),
        (MIDDLE, [*CLOSE, *AFTER], CLOSE, close_in),
        (EARLY, [*FAR, *CLOSE], FAR, far_in),
    ):
        *own, strips = call(
            outer_kernel(rows, places, arrived), [SMEM] * 3 + [VMEM] * 4,
            [shape(len(rows), share, *piece)] * 4 + [shape(*strips.shape)],
            (*tables, halo, left, partial, strips), flops=work * len(rows) // 2, aliases={6: 4},
        )
        parts.append([own[0], *(across(own[b], b) for b in (1, 2, 3))])

    result = shape(ROWS, share, 128, 128, dtype=jnp.float32)
    scratch = [
        pltpu.VMEM((ROWS, share, 128, 128), density.dtype),
        pltpu.VMEM((ROWS, share, 128, 128), jnp.float32),
        pltpu.SemaphoreType.DMA((ROWS,)),
    ]
    out = call(
        final_kernel((LATE, MIDDLE), False), [SMEM] + [VMEM] * 8, [result], (meta, *parts[0], *parts[1]),
        scratch, out_specs=[ANY],
    )[0]
    return call(
        final_kernel((EARLY,), True), [SMEM] + [VMEM] * 4 + [ANY], [result], (meta, *parts[2], out),
        scratch, out_specs=[ANY], aliases={5: 0},
    )[0]


def solution(mesh):
    in_specs = (P(("row", "layer"), None, "col", None), P(), P(), P())
    out_specs = P(("row", "layer"), "col", None, None)
    return jax.shard_map(
        per_device, mesh=mesh, in_specs=in_specs, out_specs=out_specs, check_vma=False
    )
```

```python
import jax
import jax.numpy as jnp
from jax import lax
from jax.experimental import pallas as pl
from jax.experimental.pallas import tpu as pltpu
from jax.sharding import PartitionSpec as P

RADIUS = 5
BAND = 2 * RADIUS + 1
ROWS = 8
NEAR = ROWS + 2 * RADIUS
STRIPS = ROWS + 4 * RADIUS
REACH = ROWS + 6 * RADIUS
NT = (((1,), (1,)), ((), ()))
VMEM = pl.BlockSpec(memory_space=pltpu.VMEM)
SMEM = pl.BlockSpec(memory_space=pltpu.SMEM)
ANY = pl.BlockSpec(memory_space=pl.ANY)
HBM = pl.BlockSpec(memory_space=pltpu.HBM)

SHIFTS = (1, -1, 2, -2)
OWN = [(j, o) for j in range(ROWS) for o in range(BAND)]
LISTS = (
    [(j, o) for j, o in OWN if ROWS <= j + o <= ROWS + RADIUS - 1],
    [(j, o) for j, o in OWN if RADIUS <= j + o <= 2 * RADIUS - 1],
    [(j, o) for j, o in OWN if j + o >= 2 * ROWS],
    [(j, o) for j, o in OWN if j + o < BAND - 1 - ROWS],
)
EDGES = (
    [(m, o) for m, o in OWN if m + o < RADIUS],
    [(m, o) for m, o in OWN if m + o >= RADIUS + ROWS],
)
LATE = range(ROWS - RADIUS, ROWS)
EARLY = range(0, ROWS - RADIUS)
AFTER = range(RADIUS + ROWS, NEAR)
CLOSE = range(ROWS - RADIUS, RADIUS)
FAR = range(0, ROWS - RADIUS)
RELAY = 3


def wrapped(value, total):
    return jnp.where(value < 0, value + total, jnp.where(value >= total, value - total, value))


def offset_slot(pattern, i, s, first):
    listed = pattern[s, first + i]
    o = wrapped(listed - (first + i) + RADIUS, pattern.shape[1])
    return jnp.where(listed >= 0, o, BAND)


def position(pattern, i, s, first):
    o = offset_slot(pattern, i, s, first)
    return jnp.where(o < BAND, i + o, (i + BAND) % NEAR)


def reorder_kernel(meta, pattern, density, h0, h1, h2, h3, band, blocks, table, sems):
    first = meta[1]
    copies = (
        pltpu.make_async_copy(density, blocks, sems.at[0]),
        pltpu.make_async_copy(pattern, table, sems.at[1]),
    )
    for copy in copies:
        copy.start()
    band[...] = jnp.zeros_like(band)
    for copy in copies:
        copy.wait()
    for i in range(ROWS):
        for s in range(blocks.shape[1]):
            band[i, offset_slot(table, i, s, first)] = blocks[i, s]
    for out, entries in zip((h0, h1, h2, h3), LISTS):
        for e, (j, o) in enumerate(entries):
            out[e] = band[j, o]


def place(left, piece, n, p, s, col, b, i=None):
    left[n if i is None else i, p, pl.ds(pl.multiple_of((col ^ b) * 32, 32), 32), :] = piece[n, s]


def prepare_kernel(meta, pattern, l0, l1, strips, left):
    col, first = meta[0], meta[1]
    strips[...] = jnp.zeros_like(strips)
    left[...] = jnp.zeros_like(left)
    for i in range(ROWS):
        for s in range(l0.shape[1]):
            p = position(pattern, i, s, first)
            place(left, l0, i, p, s, col, 0)
            place(left, l1, i, p, s, col, 1)
            strips[i + 2 * RADIUS, p] = l0[i, s]


def relay_kernel(meta, pattern, l2, left_in, left, *pieces):
    del left_in
    col, first = meta[0], meta[1]
    for i in range(ROWS):
        piece, n = pieces[i // RELAY], i % RELAY
        for s in range(l2.shape[1]):
            place(left, l2, i, position(pattern, i, s, first), s, col, 2)
        piece[n] = l2[i]


def complete_kernel(meta, pattern, *refs):
    pieces, (strips, left) = refs[:-4], refs[-2:]
    col, first = meta[0], meta[1]
    for i in range(ROWS):
        piece, n = pieces[i // RELAY], i % RELAY
        for s in range(piece.shape[1]):
            place(left, piece, n, position(pattern, i, s, first), s, col, 3, i)
    shape = (32, 128)
    pick = lax.broadcasted_iota(jnp.int32, shape, 1) == lax.broadcasted_iota(jnp.int32, shape, 0) + col * 32
    pick = pick.astype(left.dtype)
    for edge in EDGES:
        blocks = jnp.concatenate([left[m, m + o] for m, o in edge], axis=0)
        turned = lax.dot_general(pick, blocks, NT, preferred_element_type=jnp.float32)
        for e, (m, o) in enumerate(edge):
            strips[m + o + RADIUS, m + RADIUS] = turned[:, e * 128 : (e + 1) * 128].astype(strips.dtype)


def gather_dot(strips, left, targets, i, places):
    w = jnp.concatenate([left[i, p] for p in places], axis=1)
    rows = [jnp.concatenate([strips[t, p] for p in places], axis=1) for t in targets]
    x = jnp.concatenate(rows, axis=0)
    return lax.dot_general(x, w, NT, preferred_element_type=jnp.float32)


def square_row(kept, strips, left, i, first):
    total = kept.shape[1]
    targets = [wrapped(kept[s, first + i] - first + 2 * RADIUS, total) for s in range(kept.shape[0])]
    acc = gather_dot(strips, left, targets, i, range(i, i + BAND))
    return acc.reshape(len(targets), 32, 128).astype(strips.dtype)


def low_kernel(meta, kept, h0, h1, h2, h3, left, strips_in, low, strips):
    del strips_in
    first = meta[1]
    for halo, entries, shift in zip((h0, h1, h2, h3), LISTS, SHIFTS):
        for e, (j, o) in enumerate(entries):
            row = j - shift * ROWS
            strips[row + 2 * RADIUS, row + o] = halo[e]
    for i in range(RADIUS):
        low[i] = square_row(kept, strips, left, i, first)


def high_kernel(meta, kept, low, strips, left, far, close):
    first = meta[1]
    for i in range(RADIUS, ROWS):
        row = square_row(kept, strips, left, i, first)
        if i < ROWS - len(CLOSE):
            far[i - ROWS + RADIUS] = row
        else:
            close[i - ROWS + len(CLOSE)] = row
    for i in range(ROWS - RADIUS, RADIUS):
        far[i - ROWS + RADIUS] = low[i]


def strip_of(table, s, row, first):
    total = table.shape[1]
    return wrapped(table[s, wrapped(row, total)] - first + 3 * RADIUS, total)


def cube_targets(cube, i, col, first, share):
    return [strip_of(cube, (col ^ b) * share + q, first + i, first) for b in range(4) for q in range(share)]


def insert_rows(strips, kept, rows, places, first):
    for k, p in enumerate(places):
        for s in range(rows.shape[1]):
            strips[strip_of(kept, s, first - RADIUS + p, first), p] = rows[k, s]


def inner_kernel(meta, kept, cube, low, far, close, left, strips, partial):
    col, first = meta[0], meta[1]
    strips[...] = jnp.zeros_like(strips)
    insert_rows(strips, kept, low, range(RADIUS, 2 * RADIUS), first)
    insert_rows(strips, kept, far, range(ROWS, ROWS + len(FAR)), first)
    insert_rows(strips, kept, close, range(RADIUS + ROWS - len(CLOSE), RADIUS + ROWS), first)
    share = cube.shape[0] // 4

    @pl.loop(0, ROWS)
    def _(i):
        targets = cube_targets(cube, i, col, first, share)
        acc = gather_dot(strips, left, targets, i, range(RADIUS, RADIUS + ROWS))
        for e, t in enumerate(targets):
            mine = strips[t, i + RADIUS].astype(jnp.float32)
            partial[i, e] = 3.0 * mine - 2.0 * acc[e * 32 : (e + 1) * 32]


def outer_kernel(rows, places, arrived):
    def kernel(meta, kept, cube, *refs):
        halos, (left, partial, _, o0, o1, o2, o3, strips) = refs[:-8], refs[-8:]
        col, first = meta[0], meta[1]
        for halo, span in zip(halos, arrived):
            insert_rows(strips, kept, halo, span, first)
        share = cube.shape[0] // 4
        for n, i in enumerate(rows):
            targets = cube_targets(cube, i, col, first, share)
            acc = gather_dot(strips, left, targets, i, [p for p in places if i <= p < i + BAND])
            for e in range(len(targets)):
                piece = partial[i, e] - 2.0 * acc[e * 32 : (e + 1) * 32]
                (o0, o1, o2, o3)[e // share][n, e % share] = piece.astype(o0.dtype)

    return kernel


def final_kernel(rows):
    def kernel(meta, *refs):
        col = meta[0]
        out, whole, turned, sems = refs[-4:]
        for b, p in enumerate(refs[:4]):
            whole[:, :, pl.ds(pl.multiple_of((col ^ b) * 32, 32), 32), :] = p[...]
        copies = []
        for n, i in enumerate(rows):
            for q in range(out.shape[1]):
                turned[n, q] = whole[n, q].T.astype(turned.dtype)
            copies.append(pltpu.make_async_copy(turned.at[n], out.at[i], sems.at[n]))
            copies[-1].start()
        for copy in copies:
            copy.wait()

    return kernel


def shape(*dims, dtype=jnp.bfloat16):
    return jax.ShapeDtypeStruct(dims, dtype)


def call(kernel, specs, outs, args, scratch=(), flops=0, aliases=None, out_specs=None, limit=16):
    size = sum(a.size * a.dtype.itemsize for a in args) + sum(o.size * o.dtype.itemsize for o in outs)
    return pl.pallas_call(
        kernel,
        out_shape=outs,
        in_specs=specs,
        out_specs=out_specs or [VMEM] * len(outs),
        scratch_shapes=scratch,
        input_output_aliases=aliases or {},
        compiler_params=pltpu.CompilerParams(vmem_limit_bytes=limit << 20),
        cost_estimate=pl.CostEstimate(flops=flops, bytes_accessed=size, transcendentals=0),
    )(*args)


def per_device(density, pattern, square_filter, cube_filter):
    layers = lax.axis_size("layer")
    groups = lax.axis_size("row") * layers
    assert density.shape[0] == ROWS and lax.axis_size("col") == 4
    piece = density.shape[2:]
    col = lax.axis_index("col")
    first = (lax.axis_index("row") * layers + lax.axis_index("layer")) * ROWS
    meta = jnp.stack([col, first]).astype(jnp.int32)
    pattern, kept, cube = pattern.T, square_filter.T, cube_filter.T
    width, slots = kept.shape[0], cube.shape[0]
    share = slots // 4

    def shifted(x, d):
        return lax.ppermute(x, ("row", "layer"), [(g, (g + d) % groups) for g in range(groups)])

    def across(x, bits):
        return lax.ppermute(x, "col", [(c, c ^ bits) for c in range(4)])

    l2 = across(density, 2)
    l1 = across(density, 1)
    payload = call(
        reorder_kernel, [SMEM, HBM, HBM], [shape(len(e), *piece) for e in LISTS], (meta, pattern, density),
        [pltpu.VMEM((ROWS, BAND + 1, *piece), density.dtype), pltpu.VMEM(density.shape, density.dtype),
         pltpu.SMEM(pattern.shape, pattern.dtype), pltpu.SemaphoreType.DMA((2,))],
    )
    payload, l1 = lax.optimization_barrier((payload, l1))
    halos = [shifted(p, d) for p, d in zip(payload, SHIFTS)]
    strips, left = call(
        prepare_kernel, [SMEM] * 2 + [VMEM] * 2,
        [shape(STRIPS, NEAR, *piece), shape(ROWS, NEAR, 128, 128)], (meta, pattern, density, l1),
    )
    l2, left, halos[2:] = lax.optimization_barrier((l2, left, halos[2:]))
    sizes = [min(RELAY, ROWS - i) for i in range(0, ROWS, RELAY)]
    left, *pieces = call(
        relay_kernel, [SMEM] * 2 + [VMEM] * 2,
        [shape(*left.shape), *(shape(n, *density.shape[1:]) for n in sizes)], (meta, pattern, l2, left),
        aliases={3: 0},
    )
    pieces = [across(p, 1) for p in pieces]
    both = [shape(*strips.shape), shape(*left.shape)]
    strips, left = call(
        complete_kernel, [SMEM] * 2 + [VMEM] * (len(pieces) + 2), both, (meta, pattern, *pieces, strips, left),
        aliases={2 + len(pieces): 0, 3 + len(pieces): 1},
    )
    work = 2 * width * BAND * 128 * 128 * 32
    low, strips = call(
        low_kernel, [SMEM] * 2 + [VMEM] * 6, [shape(RADIUS, width, *piece), both[0]],
        (meta, kept, *halos, left, strips), flops=work * RADIUS, aliases={7: 1},
    )
    after = shifted(low, -1)
    far, close = call(
        high_kernel, [SMEM] * 2 + [VMEM] * 3,
        [shape(len(FAR), width, *piece), shape(len(CLOSE), width, *piece)],
        (meta, kept, low, strips, left), flops=work * (ROWS - RADIUS),
    )
    tables = (meta, kept, cube)
    strips, partial = call(
        inner_kernel, [SMEM] * 3 + [VMEM] * 4,
        [shape(REACH, NEAR, *piece), shape(ROWS, slots, *piece, dtype=jnp.float32)],
        (*tables, low, far, close, left), flops=2 * slots * ROWS * ROWS * 128 * 128 * 32,
    )
    close_in = shifted(close, 1)
    far, after, close_in, partial = lax.optimization_barrier((far, after, close_in, partial))
    far_in = shifted(far, 1)

    def rest(rows, places, halos, partial, strips):
        *own, strips = call(
            outer_kernel(rows, places, [p for p, _ in halos]), [SMEM] * 3 + [VMEM] * (3 + len(halos)),
            [shape(len(rows), share, *piece)] * 4 + [shape(*strips.shape)],
            (*tables, *(h for _, h in halos), left, partial, strips), flops=work * len(rows) // 2,
            aliases={5 + len(halos): 4},
        )
        return [own[0], *(across(own[b], b) for b in (1, 2, 3))], strips

    late, strips = rest(LATE, [*CLOSE, *AFTER], ((AFTER, after), (CLOSE, close_in)), partial, strips)
    late, partial = lax.optimization_barrier((late, partial))
    early, _ = rest(EARLY, [*FAR, *CLOSE], ((FAR, far_in),), partial, strips)

    result = shape(ROWS, share, 128, 128, dtype=jnp.float32)

    def scratch(rows):
        block = (len(rows), share, 128, 128)
        return [pltpu.VMEM(block, density.dtype), pltpu.VMEM(block, jnp.float32),
                pltpu.SemaphoreType.DMA((len(rows),))]

    out = call(
        final_kernel(LATE), [SMEM] + [VMEM] * 4, [result], (meta, *late),
        scratch(LATE), out_specs=[ANY],
    )[0]
    return call(
        final_kernel(EARLY), [SMEM] + [VMEM] * 4 + [ANY], [result], (meta, *early, out),
        scratch(EARLY), out_specs=[ANY], aliases={5: 0},
    )[0]


def solution(mesh):
    in_specs = (P(("row", "layer"), None, "col", None), P(), P(), P())
    out_specs = P(("row", "layer"), "col", None, None)
    return jax.shard_map(
        per_device, mesh=mesh, in_specs=in_specs, out_specs=out_specs, check_vma=False
    )
```

```python
import jax
import jax.numpy as jnp
from jax import lax
from jax.experimental import pallas as pl
from jax.experimental.pallas import tpu as pltpu
from jax.sharding import PartitionSpec as P

RADIUS = 5
BAND = 2 * RADIUS + 1
ROWS = 8
NEAR = ROWS + 2 * RADIUS
STRIPS = ROWS + 4 * RADIUS
REACH = ROWS + 6 * RADIUS
NT = (((1,), (1,)), ((), ()))
VMEM = pl.BlockSpec(memory_space=pltpu.VMEM)
SMEM = pl.BlockSpec(memory_space=pltpu.SMEM)
ANY = pl.BlockSpec(memory_space=pl.ANY)

SHIFTS = (1, -1, 2, -2)
OWN = [(j, o) for j in range(ROWS) for o in range(BAND)]
LISTS = (
    [(j, o) for j, o in OWN if ROWS <= j + o <= ROWS + RADIUS - 1],
    [(j, o) for j, o in OWN if RADIUS <= j + o <= 2 * RADIUS - 1],
    [(j, o) for j, o in OWN if j + o >= 2 * ROWS],
    [(j, o) for j, o in OWN if j + o < BAND - 1 - ROWS],
)
EDGES = (
    [(m, o) for m, o in OWN if m + o < RADIUS],
    [(m, o) for m, o in OWN if m + o >= RADIUS + ROWS],
)
UPPER = [(j, o) for j, o in OWN if o >= RADIUS or j + o < RADIUS]
LOWER = [(m, j) for m in range(ROWS) for j in range(m + 1, min(ROWS, m + RADIUS + 1))]
LATE = range(ROWS - RADIUS, ROWS)
EARLY = range(0, ROWS - RADIUS)
AFTER = range(RADIUS + ROWS, NEAR)
CLOSE = range(ROWS - RADIUS, RADIUS)
FAR = range(0, ROWS - RADIUS)
RELAY = 21


def wrapped(value, total):
    return jnp.where(value < 0, value + total, jnp.where(value >= total, value - total, value))


def reorder_kernel(meta, pattern, density, h0, h1, h2, h3, upper, band):
    first, total = meta[1], pattern.shape[1]
    band[...] = jnp.zeros_like(band)
    for i in range(ROWS):
        for s in range(density.shape[1]):
            listed = pattern[s, first + i]
            o = wrapped(listed - (first + i) + RADIUS, total)
            band[i, jnp.where(listed >= 0, o, BAND)] = density[i, s]
    for out, entries in zip((h0, h1, h2, h3, upper), (*LISTS, UPPER)):
        for e, (j, o) in enumerate(entries):
            out[e] = band[j, o]


def place(left, piece, entries, col, b):
    start = pl.multiple_of((col ^ b) * 32, 32)
    for e, (i, o) in enumerate(entries):
        left[i, i + o, pl.ds(start, 32), :] = piece[e]


def prepare_kernel(meta, band, upper, u1, strips, left):
    strips[...] = jnp.zeros_like(strips)
    left[...] = jnp.zeros_like(left)
    for i in range(ROWS):
        strips[i + 2 * RADIUS, i : i + BAND] = band[i, :BAND]
    place(left, upper, UPPER, meta[0], 0)
    place(left, u1, UPPER, meta[0], 1)


def relay_kernel(u2, *pieces):
    for n, piece in enumerate(pieces):
        piece[...] = u2[n * RELAY : n * RELAY + piece.shape[0]]


def place_kernel(meta, u2, left_in, left):
    del left_in
    place(left, u2, UPPER, meta[0], 2)


def complete_kernel(meta, *refs):
    pieces, (strips, left) = refs[:-4], refs[-2:]
    col = meta[0]
    for n, piece in enumerate(pieces):
        place(left, piece, UPPER[n * RELAY : n * RELAY + piece.shape[0]], col, 3)
    shape = (32, 128)
    pick = lax.broadcasted_iota(jnp.int32, shape, 1) == lax.broadcasted_iota(jnp.int32, shape, 0) + col * 32
    pick = pick.astype(left.dtype)
    for edge in EDGES:
        blocks = jnp.concatenate([left[m, m + o] for m, o in edge], axis=0)
        turned = lax.dot_general(pick, blocks, NT, preferred_element_type=jnp.float32)
        for e, (m, o) in enumerate(edge):
            strips[m + o + RADIUS, m + RADIUS] = turned[:, e * 128 : (e + 1) * 128].astype(strips.dtype)
    for m, j in LOWER:
        left[j, m + RADIUS] = left[m, j + RADIUS].T


def gather_dot(strips, left, targets, i, places):
    w = jnp.concatenate([left[i, p] for p in places], axis=1)
    rows = [jnp.concatenate([strips[t, p] for p in places], axis=1) for t in targets]
    x = jnp.concatenate(rows, axis=0)
    return lax.dot_general(x, w, NT, preferred_element_type=jnp.float32)


def square_row(kept, strips, left, i, first):
    total = kept.shape[1]
    targets = [wrapped(kept[s, first + i] - first + 2 * RADIUS, total) for s in range(kept.shape[0])]
    acc = gather_dot(strips, left, targets, i, range(i, i + BAND))
    return acc.reshape(len(targets), 32, 128).astype(strips.dtype)


def low_kernel(meta, kept, h0, h1, h2, h3, left, strips_in, low, strips):
    del strips_in
    first = meta[1]
    for halo, entries, shift in zip((h0, h1, h2, h3), LISTS, SHIFTS):
        for e, (j, o) in enumerate(entries):
            row = j - shift * ROWS
            strips[row + 2 * RADIUS, row + o] = halo[e]
    for i in range(RADIUS):
        low[i] = square_row(kept, strips, left, i, first)


def high_kernel(meta, kept, low, strips, left, far, close):
    first = meta[1]
    for i in range(RADIUS, ROWS):
        row = square_row(kept, strips, left, i, first)
        if i < ROWS - len(CLOSE):
            far[i - ROWS + RADIUS] = row
        else:
            close[i - ROWS + len(CLOSE)] = row
    for i in range(ROWS - RADIUS, RADIUS):
        far[i - ROWS + RADIUS] = low[i]


def strip_of(table, s, row, first):
    total = table.shape[1]
    return wrapped(table[s, wrapped(row, total)] - first + 3 * RADIUS, total)


def cube_targets(cube, i, col, first, share):
    return [strip_of(cube, (col ^ b) * share + q, first + i, first) for b in range(4) for q in range(share)]


def insert_rows(strips, kept, rows, places, first):
    for k, p in enumerate(places):
        for s in range(rows.shape[1]):
            strips[strip_of(kept, s, first - RADIUS + p, first), p] = rows[k, s]


def inner_kernel(meta, kept, cube, low, far, close, left, strips, partial):
    col, first = meta[0], meta[1]
    strips[...] = jnp.zeros_like(strips)
    insert_rows(strips, kept, low, range(RADIUS, 2 * RADIUS), first)
    insert_rows(strips, kept, far, range(ROWS, ROWS + len(FAR)), first)
    insert_rows(strips, kept, close, range(RADIUS + ROWS - len(CLOSE), RADIUS + ROWS), first)
    share = cube.shape[0] // 4

    @pl.loop(0, ROWS)
    def _(i):
        targets = cube_targets(cube, i, col, first, share)
        acc = gather_dot(strips, left, targets, i, range(RADIUS, RADIUS + ROWS))
        for e, t in enumerate(targets):
            mine = strips[t, i + RADIUS].astype(jnp.float32)
            partial[i, e] = 3.0 * mine - 2.0 * acc[e * 32 : (e + 1) * 32]


def outer_kernel(rows, places, arrived):
    def kernel(meta, kept, cube, *refs):
        halos, (left, partial, _, o0, o1, o2, o3, strips) = refs[:-8], refs[-8:]
        col, first = meta[0], meta[1]
        for halo, span in zip(halos, arrived):
            insert_rows(strips, kept, halo, span, first)
        share = cube.shape[0] // 4
        for n, i in enumerate(rows):
            targets = cube_targets(cube, i, col, first, share)
            acc = gather_dot(strips, left, targets, i, [p for p in places if i <= p < i + BAND])
            for e in range(len(targets)):
                piece = partial[i, e] - 2.0 * acc[e * 32 : (e + 1) * 32]
                (o0, o1, o2, o3)[e // share][n, e % share] = piece.astype(o0.dtype)

    return kernel


def final_kernel(rows):
    def kernel(meta, *refs):
        col = meta[0]
        out, whole, turned, sems = refs[-4:]
        for b, p in enumerate(refs[:4]):
            whole[:, :, pl.ds(pl.multiple_of((col ^ b) * 32, 32), 32), :] = p[...]
        copies = []
        for n, i in enumerate(rows):
            for q in range(out.shape[1]):
                turned[n, q] = whole[n, q].T.astype(turned.dtype)
            copies.append(pltpu.make_async_copy(turned.at[n], out.at[i], sems.at[n]))
            copies[-1].start()
        for copy in copies:
            copy.wait()

    return kernel


def shape(*dims, dtype=jnp.bfloat16):
    return jax.ShapeDtypeStruct(dims, dtype)


def call(kernel, specs, outs, args, scratch=(), flops=0, aliases=None, out_specs=None, limit=16, free=False):
    size = sum(a.size * a.dtype.itemsize for a in args) + sum(o.size * o.dtype.itemsize for o in outs)
    size = 0 if free else size
    return pl.pallas_call(
        kernel,
        out_shape=outs,
        in_specs=specs,
        out_specs=out_specs or [VMEM] * len(outs),
        scratch_shapes=scratch,
        input_output_aliases=aliases or {},
        compiler_params=pltpu.CompilerParams(vmem_limit_bytes=limit << 20),
        cost_estimate=pl.CostEstimate(flops=flops, bytes_accessed=size, transcendentals=0),
    )(*args)


def per_device(density, pattern, square_filter, cube_filter):
    layers = lax.axis_size("layer")
    groups = lax.axis_size("row") * layers
    assert density.shape[0] == ROWS and lax.axis_size("col") == 4
    piece = density.shape[2:]
    col = lax.axis_index("col")
    first = (lax.axis_index("row") * layers + lax.axis_index("layer")) * ROWS
    meta = jnp.stack([col, first]).astype(jnp.int32)
    pattern, kept, cube = pattern.T, square_filter.T, cube_filter.T
    width, slots = kept.shape[0], cube.shape[0]
    share = slots // 4

    def shifted(x, d):
        return lax.ppermute(x, ("row", "layer"), [(g, (g + d) % groups) for g in range(groups)])

    def across(x, bits):
        return lax.ppermute(x, "col", [(c, c ^ bits) for c in range(4)])

    *halos, upper, band = call(
        reorder_kernel, [SMEM, SMEM, VMEM],
        [*(shape(len(e), *piece) for e in (*LISTS, UPPER)), shape(ROWS, BAND + 1, *piece)],
        (meta, pattern, density),
    )
    u2 = across(upper, 2)
    u1 = across(upper, 1)
    halos = [shifted(p, d) for p, d in zip(halos, SHIFTS)]
    strips, left = call(
        prepare_kernel, [SMEM] + [VMEM] * 3,
        [shape(STRIPS, NEAR, *piece), shape(ROWS, NEAR, 128, 128)], (meta, band, upper, u1),
    )
    u2, left, halos[2:] = lax.optimization_barrier((u2, left, halos[2:]))
    sizes = [min(RELAY, len(UPPER) - e) for e in range(0, len(UPPER), RELAY)]
    pieces = call(relay_kernel, [VMEM], [shape(n, *piece) for n in sizes], (u2,))
    pieces = [across(p, 1) for p in pieces]
    left = call(place_kernel, [SMEM] + [VMEM] * 2, [shape(*left.shape)], (meta, u2, left), aliases={2: 0})[0]
    both = [shape(*strips.shape), shape(*left.shape)]
    strips, left = call(
        complete_kernel, [SMEM] + [VMEM] * (len(pieces) + 2), both, (meta, *pieces, strips, left),
        aliases={1 + len(pieces): 0, 2 + len(pieces): 1},
    )
    work = 2 * width * BAND * 128 * 128 * 32
    low, strips = call(
        low_kernel, [SMEM] * 2 + [VMEM] * 6, [shape(RADIUS, width, *piece), both[0]],
        (meta, kept, *halos, left, strips), flops=work * RADIUS, aliases={7: 1},
    )
    after = shifted(low, -1)
    far, close = call(
        high_kernel, [SMEM] * 2 + [VMEM] * 3,
        [shape(len(FAR), width, *piece), shape(len(CLOSE), width, *piece)],
        (meta, kept, low, strips, left), flops=work * (ROWS - RADIUS),
    )
    tables = (meta, kept, cube)
    strips, partial = call(
        inner_kernel, [SMEM] * 3 + [VMEM] * 4,
        [shape(REACH, NEAR, *piece), shape(ROWS, slots, *piece, dtype=jnp.float32)],
        (*tables, low, far, close, left), flops=2 * slots * ROWS * ROWS * 128 * 128 * 32,
    )
    close_in = shifted(close, 1)
    far, after, partial = lax.optimization_barrier((far, after, partial))
    far_in = shifted(far, 1)

    def rest(rows, places, halos, partial, strips):
        *own, strips = call(
            outer_kernel(rows, places, [p for p, _ in halos]), [SMEM] * 3 + [VMEM] * (3 + len(halos)),
            [shape(len(rows), share, *piece)] * 4 + [shape(*strips.shape)],
            (*tables, *(h for _, h in halos), left, partial, strips), aliases={5 + len(halos): 4}, free=True,
        )
        return [own[0], *(across(own[b], b) for b in (1, 2, 3))], strips

    late, strips = rest(LATE, [*CLOSE, *AFTER], ((AFTER, after), (CLOSE, close_in)), partial, strips)
    early, _ = rest(EARLY, [*FAR, *CLOSE], ((FAR, far_in),), partial, strips)

    result = shape(ROWS, share, 128, 128, dtype=jnp.float32)

    def scratch(rows):
        block = (len(rows), share, 128, 128)
        return [pltpu.VMEM(block, density.dtype), pltpu.VMEM(block, jnp.float32),
                pltpu.SemaphoreType.DMA((len(rows),))]

    out = call(
        final_kernel(LATE), [SMEM] + [VMEM] * 4, [result], (meta, *late),
        scratch(LATE), out_specs=[ANY],
    )[0]
    return call(
        final_kernel(EARLY), [SMEM] + [VMEM] * 4 + [ANY], [result], (meta, *early, out),
        scratch(EARLY), out_specs=[ANY], aliases={5: 0},
    )[0]


def solution(mesh):
    in_specs = (P(("row", "layer"), None, "col", None), P(), P(), P())
    out_specs = P(("row", "layer"), "col", None, None)
    return jax.shard_map(
        per_device, mesh=mesh, in_specs=in_specs, out_specs=out_specs, check_vma=False
    )
```

```python
import jax
import jax.numpy as jnp
from jax import lax
from jax.experimental import pallas as pl
from jax.experimental.pallas import tpu as pltpu
from jax.sharding import PartitionSpec as P

RADIUS = 5
BAND = 2 * RADIUS + 1
ROWS = 8
NEAR = ROWS + 2 * RADIUS
STRIPS = ROWS + 4 * RADIUS
REACH = ROWS + 6 * RADIUS
NT = (((1,), (1,)), ((), ()))
VMEM = pl.BlockSpec(memory_space=pltpu.VMEM)
SMEM = pl.BlockSpec(memory_space=pltpu.SMEM)
ANY = pl.BlockSpec(memory_space=pl.ANY)

SHIFTS = (1, -1, 2, -2)
OWN = [(j, o) for j in range(ROWS) for o in range(BAND)]
LISTS = (
    [(j, o) for j, o in OWN if ROWS <= j + o <= ROWS + RADIUS - 1],
    [(j, o) for j, o in OWN if RADIUS <= j + o <= 2 * RADIUS - 1],
    [(j, o) for j, o in OWN if j + o >= 2 * ROWS],
    [(j, o) for j, o in OWN if j + o < BAND - 1 - ROWS],
)
EDGES = (
    [(m, o) for m, o in OWN if m + o < RADIUS],
    [(m, o) for m, o in OWN if m + o >= RADIUS + ROWS],
)
UPPER = [(j, o) for j, o in OWN if o >= RADIUS or j + o < RADIUS]
LOWER = [(m, j) for m in range(ROWS) for j in range(m + 1, min(ROWS, m + RADIUS + 1))]
EARLY = range(0, 2 * RADIUS - ROWS)
LATE = range(2 * RADIUS - ROWS, ROWS)
AFTER = range(RADIUS + ROWS, NEAR)
CLOSE = range(2 * RADIUS - ROWS, RADIUS)
FAR = range(0, 2 * RADIUS - ROWS)
RELAY = 21


def wrapped(value, total):
    if total & (total - 1) == 0:
        return value & (total - 1)
    return jnp.where(value < 0, value + total, jnp.where(value >= total, value - total, value))


def reorder_kernel(meta, pattern, density, h0, h1, h2, h3, upper, band):
    first, total = meta[1], pattern.shape[1]
    band[...] = jnp.zeros_like(band)
    for i in range(ROWS):
        for s in range(density.shape[1]):
            listed = pattern[s, first + i]
            o = wrapped(listed - (first + i) + RADIUS, total)
            band[i, jnp.where(listed >= 0, o, BAND)] = density[i, s]
    for out, entries in zip((h0, h1, h2, h3, upper), (*LISTS, UPPER)):
        for e, (j, o) in enumerate(entries):
            out[e] = band[j, o]


def place(left, piece, entries, col, b):
    start = pl.multiple_of((col ^ b) * 32, 32)
    for e, (i, o) in enumerate(entries):
        left[i, i + o, pl.ds(start, 32), :] = piece[e]


def prepare_kernel(meta, band, upper, u1, strips, left):
    strips[...] = jnp.zeros_like(strips)
    left[...] = jnp.zeros_like(left)
    for i in range(ROWS):
        strips[i + 2 * RADIUS, i : i + BAND] = band[i, :BAND]
    place(left, upper, UPPER, meta[0], 0)
    place(left, u1, UPPER, meta[0], 1)


def relay_kernel(u2, *pieces):
    for n, piece in enumerate(pieces):
        piece[...] = u2[n * RELAY : n * RELAY + piece.shape[0]]


def place_kernel(meta, u2, left_in, left):
    del left_in
    place(left, u2, UPPER, meta[0], 2)


def complete_kernel(meta, *refs):
    pieces, (strips, left) = refs[:-4], refs[-2:]
    col = meta[0]
    for n, piece in enumerate(pieces):
        place(left, piece, UPPER[n * RELAY : n * RELAY + piece.shape[0]], col, 3)
    shape = (32, 128)
    pick = lax.broadcasted_iota(jnp.int32, shape, 1) == lax.broadcasted_iota(jnp.int32, shape, 0) + col * 32
    pick = pick.astype(left.dtype)
    for edge in EDGES:
        blocks = jnp.concatenate([left[m, m + o] for m, o in edge], axis=0)
        turned = lax.dot_general(pick, blocks, NT, preferred_element_type=jnp.float32)
        for e, (m, o) in enumerate(edge):
            strips[m + o + RADIUS, m + RADIUS] = turned[:, e * 128 : (e + 1) * 128].astype(strips.dtype)
    for m, j in LOWER:
        left[j, m + RADIUS] = left[m, j + RADIUS].T


def gather_dot(strips, left, targets, i, places):
    w = jnp.concatenate([left[i, p] for p in places], axis=1)
    rows = [jnp.concatenate([strips[t, p] for p in places], axis=1) for t in targets]
    x = jnp.concatenate(rows, axis=0)
    return lax.dot_general(x, w, NT, preferred_element_type=jnp.float32)


def square_row(kept, strips, left, i, first):
    total = kept.shape[1]
    targets = [wrapped(kept[s, first + i] - first + 2 * RADIUS, total) for s in range(kept.shape[0])]
    acc = gather_dot(strips, left, targets, i, range(i, i + BAND))
    return acc.reshape(len(targets), 32, 128).astype(strips.dtype)


def low_kernel(meta, kept, h0, h1, h2, h3, left, strips_in, low, far, strips):
    del strips_in
    first = meta[1]
    for halo, entries, shift in zip((h0, h1, h2, h3), LISTS, SHIFTS):
        for e, (j, o) in enumerate(entries):
            row = j - shift * ROWS
            strips[row + 2 * RADIUS, row + o] = halo[e]
    for i in range(RADIUS):
        row = square_row(kept, strips, left, i, first)
        low[i] = row
        if i >= ROWS - RADIUS:
            far[i - ROWS + RADIUS] = row


def high_kernel(meta, kept, strips, left, close):
    for i in range(RADIUS, ROWS):
        close[i - RADIUS] = square_row(kept, strips, left, i, meta[1])


def strip_of(table, s, row, first):
    total = table.shape[1]
    return wrapped(table[s, wrapped(row, total)] - first + 3 * RADIUS, total)


def cube_targets(cube, i, col, first, share):
    return [strip_of(cube, (col ^ b) * share + q, first + i, first) for b in range(4) for q in range(share)]


def insert_rows(strips, kept, rows, places, first):
    for k, p in enumerate(places):
        for s in range(rows.shape[1]):
            strips[strip_of(kept, s, first - RADIUS + p, first), p] = rows[k, s]


def inner_kernel(meta, kept, cube, low, close, left, strips, partial):
    col, first = meta[0], meta[1]
    strips[...] = jnp.zeros_like(strips)
    insert_rows(strips, kept, low, range(RADIUS, 2 * RADIUS), first)
    insert_rows(strips, kept, close, range(2 * RADIUS, RADIUS + ROWS), first)
    share = cube.shape[0] // 4

    @pl.loop(0, ROWS)
    def _(i):
        targets = cube_targets(cube, i, col, first, share)
        acc = gather_dot(strips, left, targets, i, range(RADIUS, RADIUS + ROWS))
        for e, t in enumerate(targets):
            mine = strips[t, i + RADIUS].astype(jnp.float32)
            partial[i, e] = 3.0 * mine - 2.0 * acc[e * 32 : (e + 1) * 32]


def bridge_kernel(meta, kept, cube, left, partial, strips, early):
    share = cube.shape[0] // 4
    for n, i in enumerate(EARLY):
        targets = cube_targets(cube, i, meta[0], meta[1], share)
        acc = gather_dot(strips, left, targets, i, CLOSE)
        for e in range(len(targets)):
            early[n, e] = partial[i, e] - 2.0 * acc[e * 32 : (e + 1) * 32]


def outer_kernel(rows, start, places, arrived):
    def kernel(meta, kept, cube, *refs):
        halos, (left, partial, _, o0, o1, o2, o3, strips) = refs[:-8], refs[-8:]
        col, first = meta[0], meta[1]
        for halo, span in zip(halos, arrived):
            insert_rows(strips, kept, halo, span, first)
        share = cube.shape[0] // 4
        for n, i in enumerate(rows):
            targets = cube_targets(cube, i, col, first, share)
            acc = gather_dot(strips, left, targets, i, [p for p in places if i <= p < i + BAND])
            for e in range(len(targets)):
                piece = partial[i - start, e] - 2.0 * acc[e * 32 : (e + 1) * 32]
                (o0, o1, o2, o3)[e // share][n, e % share] = piece.astype(o0.dtype)

    return kernel


def final_kernel(rows):
    def kernel(meta, *refs):
        col = meta[0]
        out, whole, turned, sems = refs[-4:]
        for b, p in enumerate(refs[:4]):
            whole[:, :, pl.ds(pl.multiple_of((col ^ b) * 32, 32), 32), :] = p[...]
        copies = []
        for n, i in enumerate(rows):
            for q in range(out.shape[1]):
                turned[n, q] = whole[n, q].T.astype(turned.dtype)
            copies.append(pltpu.make_async_copy(turned.at[n], out.at[i], sems.at[n]))
            copies[-1].start()
        for copy in copies:
            copy.wait()

    return kernel


def shape(*dims, dtype=jnp.bfloat16):
    return jax.ShapeDtypeStruct(dims, dtype)


def call(kernel, specs, outs, args, scratch=(), flops=0, aliases=None, out_specs=None, limit=16, free=False):
    size = sum(a.size * a.dtype.itemsize for a in args) + sum(o.size * o.dtype.itemsize for o in outs)
    size = 0 if free else size
    return pl.pallas_call(
        kernel,
        out_shape=outs,
        in_specs=specs,
        out_specs=out_specs or [VMEM] * len(outs),
        scratch_shapes=scratch,
        input_output_aliases=aliases or {},
        compiler_params=pltpu.CompilerParams(vmem_limit_bytes=limit << 20),
        cost_estimate=pl.CostEstimate(flops=flops, bytes_accessed=size, transcendentals=0),
    )(*args)


def per_device(density, pattern, square_filter, cube_filter):
    layers = lax.axis_size("layer")
    groups = lax.axis_size("row") * layers
    assert density.shape[0] == ROWS and lax.axis_size("col") == 4
    piece = density.shape[2:]
    col = lax.axis_index("col")
    first = (lax.axis_index("row") * layers + lax.axis_index("layer")) * ROWS
    meta = jnp.stack([col, first]).astype(jnp.int32)
    pattern, kept, cube = pattern.T, square_filter.T, cube_filter.T
    width, slots = kept.shape[0], cube.shape[0]
    share = slots // 4

    def shifted(x, d):
        return lax.ppermute(x, ("row", "layer"), [(g, (g + d) % groups) for g in range(groups)])

    def across(x, bits):
        return lax.ppermute(x, "col", [(c, c ^ bits) for c in range(4)])

    *halos, upper, band = call(
        reorder_kernel, [SMEM, SMEM, VMEM],
        [*(shape(len(e), *piece) for e in (*LISTS, UPPER)), shape(ROWS, BAND + 1, *piece)],
        (meta, pattern, density),
    )
    u2 = across(upper, 2)
    u1 = across(upper, 1)
    halos = [shifted(p, d) for p, d in zip(halos, SHIFTS)]
    strips, left = call(
        prepare_kernel, [SMEM] + [VMEM] * 3,
        [shape(STRIPS, NEAR, *piece), shape(ROWS, NEAR, 128, 128)], (meta, band, upper, u1),
    )
    u2, left, halos[2:] = lax.optimization_barrier((u2, left, halos[2:]))
    sizes = [min(RELAY, len(UPPER) - e) for e in range(0, len(UPPER), RELAY)]
    pieces = call(relay_kernel, [VMEM], [shape(n, *piece) for n in sizes], (u2,))
    pieces = [across(p, 1) for p in pieces]
    left = call(place_kernel, [SMEM] + [VMEM] * 2, [shape(*left.shape)], (meta, u2, left), aliases={2: 0})[0]
    both = [shape(*strips.shape), shape(*left.shape)]
    strips, left = call(
        complete_kernel, [SMEM] + [VMEM] * (len(pieces) + 2), both, (meta, *pieces, strips, left),
        aliases={1 + len(pieces): 0, 2 + len(pieces): 1},
    )
    work = 2 * width * BAND * 128 * 128 * 32
    low, far, strips = call(
        low_kernel, [SMEM] * 2 + [VMEM] * 6,
        [shape(RADIUS, width, *piece), shape(len(FAR), width, *piece), both[0]],
        (meta, kept, *halos, left, strips), flops=work * RADIUS, aliases={7: 2},
    )
    after = shifted(low, -1)
    close = call(
        high_kernel, [SMEM] * 2 + [VMEM] * 2, [shape(len(CLOSE), width, *piece)],
        (meta, kept, strips, left), flops=work * (ROWS - RADIUS),
    )[0]
    close_in = shifted(close, 1)

    tables = (meta, kept, cube)
    strips, partial = call(
        inner_kernel, [SMEM] * 3 + [VMEM] * 3,
        [shape(REACH, NEAR, *piece), shape(ROWS, slots, *piece, dtype=jnp.float32)],
        (*tables, low, close, left), flops=2 * slots * ROWS * ROWS * 128 * 128 * 32,
    )
    far, after, partial = lax.optimization_barrier((far, after, partial))
    far_in = shifted(far, 1)

    def rest(rows, start, places, halos, partial, strips):
        *own, strips = call(
            outer_kernel(rows, start, places, [p for p, _ in halos]), [SMEM] * 3 + [VMEM] * (3 + len(halos)),
            [shape(len(rows), share, *piece)] * 4 + [shape(*strips.shape)],
            (*tables, *(h for _, h in halos), left, partial, strips), aliases={5 + len(halos): 4}, free=True,
        )
        return [own[0], *(across(own[b], b) for b in (1, 2, 3))], strips

    late, strips = rest(LATE, 0, [*CLOSE, *AFTER], ((AFTER, after), (CLOSE, close_in)), partial, strips)
    partial = call(
        bridge_kernel, [SMEM] * 3 + [VMEM] * 3, [shape(len(EARLY), slots, *piece, dtype=jnp.float32)],
        (*tables, left, partial, strips), free=True,
    )[0]
    early, _ = rest(EARLY, EARLY[0], FAR, ((FAR, far_in),), partial, strips)

    result = shape(ROWS, share, 128, 128, dtype=jnp.float32)

    def scratch(rows):
        block = (len(rows), share, 128, 128)
        return [pltpu.VMEM(block, density.dtype), pltpu.VMEM(block, jnp.float32),
                pltpu.SemaphoreType.DMA((len(rows),))]

    out = call(
        final_kernel(LATE), [SMEM] + [VMEM] * 4, [result], (meta, *late),
        scratch(LATE), out_specs=[ANY],
    )[0]
    return call(
        final_kernel(EARLY), [SMEM] + [VMEM] * 4 + [ANY], [result], (meta, *early, out),
        scratch(EARLY), out_specs=[ANY], aliases={5: 0},
    )[0]


def solution(mesh):
    in_specs = (P(("row", "layer"), None, "col", None), P(), P(), P())
    out_specs = P(("row", "layer"), "col", None, None)
    return jax.shard_map(
        per_device, mesh=mesh, in_specs=in_specs, out_specs=out_specs, check_vma=False
    )
```

```python
import jax
import jax.numpy as jnp
from jax import lax
from jax.experimental import pallas as pl
from jax.experimental.pallas import tpu as pltpu
from jax.sharding import PartitionSpec as P

RADIUS = 5
BAND = 2 * RADIUS + 1
ROWS = 8
NEAR = ROWS + 2 * RADIUS
STRIPS = ROWS + 4 * RADIUS
REACH = ROWS + 6 * RADIUS
NT = (((1,), (1,)), ((), ()))
VMEM = pl.BlockSpec(memory_space=pltpu.VMEM)
SMEM = pl.BlockSpec(memory_space=pltpu.SMEM)
ANY = pl.BlockSpec(memory_space=pl.ANY)

SHIFTS = (1, -1, 2, -2)
OWN = [(j, o) for j in range(ROWS) for o in range(BAND)]
LISTS = (
    [(j, o) for j, o in OWN if ROWS <= j + o <= ROWS + RADIUS - 1],
    [(j, o) for j, o in OWN if RADIUS <= j + o <= 2 * RADIUS - 1],
    [(j, o) for j, o in OWN if j + o >= 2 * ROWS],
    [(j, o) for j, o in OWN if j + o < BAND - 1 - ROWS],
)
EDGES = (
    [(m, o) for m, o in OWN if m + o < RADIUS],
    [(m, o) for m, o in OWN if m + o >= RADIUS + ROWS],
)
UPPER = [(j, o) for j, o in OWN if o >= RADIUS or j + o < RADIUS]
LOWER = [(m, j) for m in range(ROWS) for j in range(m + 1, min(ROWS, m + RADIUS + 1))]
EARLY = range(0, 2 * RADIUS - ROWS)
LATE = range(2 * RADIUS - ROWS, ROWS)
AFTER = range(RADIUS + ROWS, NEAR)
CLOSE = range(2 * RADIUS - ROWS, RADIUS)
FAR = range(0, 2 * RADIUS - ROWS)
RELAY = 21


def own_place():
    group = lax.axis_index("row") * lax.axis_size("layer") + lax.axis_index("layer")
    return lax.axis_index("col"), group * ROWS


def wrapped(value, total):
    if total & (total - 1) == 0:
        return value & (total - 1)
    return jnp.where(value < 0, value + total, jnp.where(value >= total, value - total, value))


def reorder_kernel(pattern, density, h0, h1, h2, h3, upper, band):
    first, total = own_place()[1], pattern.shape[1]
    band[...] = jnp.zeros_like(band)
    for i in range(ROWS):
        for s in range(density.shape[1]):
            listed = pattern[s, first + i]
            o = wrapped(listed - (first + i) + RADIUS, total)
            band[i, jnp.where(listed >= 0, o, BAND)] = density[i, s]
    for out, entries in zip((h0, h1, h2, h3, upper), (*LISTS, UPPER)):
        for e, (j, o) in enumerate(entries):
            out[e] = band[j, o]


def place(left, piece, entries, col, b):
    start = pl.multiple_of((col ^ b) * 32, 32)
    for e, (i, o) in enumerate(entries):
        left[i, i + o, pl.ds(start, 32), :] = piece[e]


def prepare_kernel(band, upper, u1, strips, left):
    strips[...] = jnp.zeros_like(strips)
    left[...] = jnp.zeros_like(left)
    for i in range(ROWS):
        strips[i + 2 * RADIUS, i : i + BAND] = band[i, :BAND]
    col = own_place()[0]
    place(left, upper, UPPER, col, 0)
    place(left, u1, UPPER, col, 1)


def relay_kernel(u2, *pieces):
    for n, piece in enumerate(pieces):
        piece[...] = u2[n * RELAY : n * RELAY + piece.shape[0]]


def place_kernel(u2, left_in, left):
    del left_in
    place(left, u2, UPPER, own_place()[0], 2)


def complete_kernel(*refs):
    pieces, (strips, left) = refs[:-4], refs[-2:]
    col = own_place()[0]
    for n, piece in enumerate(pieces):
        place(left, piece, UPPER[n * RELAY : n * RELAY + piece.shape[0]], col, 3)
    shape = (32, 128)
    pick = lax.broadcasted_iota(jnp.int32, shape, 1) == lax.broadcasted_iota(jnp.int32, shape, 0) + col * 32
    pick = pick.astype(left.dtype)
    for edge in EDGES:
        blocks = jnp.concatenate([left[m, m + o] for m, o in edge], axis=0)
        turned = lax.dot_general(pick, blocks, NT, preferred_element_type=jnp.float32)
        for e, (m, o) in enumerate(edge):
            strips[m + o + RADIUS, m + RADIUS] = turned[:, e * 128 : (e + 1) * 128].astype(strips.dtype)
    for m, j in LOWER:
        left[j, m + RADIUS] = left[m, j + RADIUS].T


def gather_dot(strips, left, targets, i, places):
    w = jnp.concatenate([left[i, p] for p in places], axis=1)
    rows = [jnp.concatenate([strips[t, p] for p in places], axis=1) for t in targets]
    x = jnp.concatenate(rows, axis=0)
    return lax.dot_general(x, w, NT, preferred_element_type=jnp.float32)


def square_row(kept, strips, left, i, first):
    total = kept.shape[1]
    targets = [wrapped(kept[s, first + i] - first + 2 * RADIUS, total) for s in range(kept.shape[0])]
    acc = gather_dot(strips, left, targets, i, range(i, i + BAND))
    return acc.reshape(len(targets), 32, 128).astype(strips.dtype)


def low_kernel(kept, h0, h1, h2, h3, left, strips_in, low, far, strips):
    del strips_in
    first = own_place()[1]
    for halo, entries, shift in zip((h0, h1, h2, h3), LISTS, SHIFTS):
        for e, (j, o) in enumerate(entries):
            row = j - shift * ROWS
            strips[row + 2 * RADIUS, row + o] = halo[e]
    for i in range(RADIUS):
        row = square_row(kept, strips, left, i, first)
        low[i] = row
        if i >= ROWS - RADIUS:
            far[i - ROWS + RADIUS] = row


def high_kernel(kept, strips, left, close):
    for i in range(RADIUS, ROWS):
        close[i - RADIUS] = square_row(kept, strips, left, i, own_place()[1])


def strip_of(table, s, row, first):
    total = table.shape[1]
    return wrapped(table[s, wrapped(row, total)] - first + 3 * RADIUS, total)


def cube_targets(cube, i, col, first, share):
    return [strip_of(cube, (col ^ b) * share + q, first + i, first) for b in range(4) for q in range(share)]


def insert_rows(strips, kept, rows, places, first):
    for k, p in enumerate(places):
        for s in range(rows.shape[1]):
            strips[strip_of(kept, s, first - RADIUS + p, first), p] = rows[k, s]


def inner_kernel(kept, cube, low, close, left, strips, partial):
    col, first = own_place()
    strips[...] = jnp.zeros_like(strips)
    insert_rows(strips, kept, low, range(RADIUS, 2 * RADIUS), first)
    insert_rows(strips, kept, close, range(2 * RADIUS, RADIUS + ROWS), first)
    share = cube.shape[0] // 4

    @pl.loop(0, ROWS)
    def _(i):
        targets = cube_targets(cube, i, col, first, share)
        acc = gather_dot(strips, left, targets, i, range(RADIUS, RADIUS + ROWS))
        for e, t in enumerate(targets):
            mine = strips[t, i + RADIUS].astype(jnp.float32)
            partial[i, e] = 3.0 * mine - 2.0 * acc[e * 32 : (e + 1) * 32]


def bridge_kernel(kept, cube, left, partial, strips, early):
    share = cube.shape[0] // 4
    for n, i in enumerate(EARLY):
        targets = cube_targets(cube, i, *own_place(), share)
        acc = gather_dot(strips, left, targets, i, CLOSE)
        for e in range(len(targets)):
            early[n, e] = partial[i, e] - 2.0 * acc[e * 32 : (e + 1) * 32]


def outer_kernel(rows, start, places, arrived):
    def kernel(kept, cube, *refs):
        halos, (left, partial, _, o0, o1, o2, o3, strips) = refs[:-8], refs[-8:]
        col, first = own_place()
        for halo, span in zip(halos, arrived):
            insert_rows(strips, kept, halo, span, first)
        share = cube.shape[0] // 4
        for n, i in enumerate(rows):
            targets = cube_targets(cube, i, col, first, share)
            acc = gather_dot(strips, left, targets, i, [p for p in places if i <= p < i + BAND])
            for e in range(len(targets)):
                piece = partial[i - start, e] - 2.0 * acc[e * 32 : (e + 1) * 32]
                (o0, o1, o2, o3)[e // share][n, e % share] = piece.astype(o0.dtype)

    return kernel


def final_kernel(rows):
    def kernel(*refs):
        col = own_place()[0]
        out, whole, turned, sems = refs[-4:]
        for b, p in enumerate(refs[:4]):
            whole[:, :, pl.ds(pl.multiple_of((col ^ b) * 32, 32), 32), :] = p[...]
        copies = []
        for n, i in enumerate(rows):
            for q in range(out.shape[1]):
                turned[n, q] = whole[n, q].T.astype(turned.dtype)
            copies.append(pltpu.make_async_copy(turned.at[n], out.at[i], sems.at[n]))
            copies[-1].start()
        for copy in copies:
            copy.wait()

    return kernel


def shape(*dims, dtype=jnp.bfloat16):
    return jax.ShapeDtypeStruct(dims, dtype)


def call(kernel, specs, outs, args, scratch=(), flops=0, aliases=None, out_specs=None, limit=16, free=False):
    size = sum(a.size * a.dtype.itemsize for a in args) + sum(o.size * o.dtype.itemsize for o in outs)
    size = 0 if free else size
    return pl.pallas_call(
        kernel,
        out_shape=outs,
        in_specs=specs,
        out_specs=out_specs or [VMEM] * len(outs),
        scratch_shapes=scratch,
        input_output_aliases=aliases or {},
        compiler_params=pltpu.CompilerParams(vmem_limit_bytes=limit << 20),
        cost_estimate=pl.CostEstimate(flops=flops, bytes_accessed=size, transcendentals=0),
    )(*args)


def per_device(density, pattern, square_filter, cube_filter):
    layers = lax.axis_size("layer")
    groups = lax.axis_size("row") * layers
    assert density.shape[0] == ROWS and lax.axis_size("col") == 4
    piece = density.shape[2:]
    pattern, kept, cube = pattern.T, square_filter.T, cube_filter.T
    width, slots = kept.shape[0], cube.shape[0]
    share = slots // 4

    def shifted(x, d):
        return lax.ppermute(x, ("row", "layer"), [(g, (g + d) % groups) for g in range(groups)])

    def across(x, bits):
        return lax.ppermute(x, "col", [(c, c ^ bits) for c in range(4)])

    *halos, upper, band = call(
        reorder_kernel, [SMEM, VMEM],
        [*(shape(len(e), *piece) for e in (*LISTS, UPPER)), shape(ROWS, BAND + 1, *piece)],
        (pattern, density),
    )
    u2 = across(upper, 2)
    u1 = across(upper, 1)
    halos = [shifted(p, d) for p, d in zip(halos, SHIFTS)]
    strips, left = call(
        prepare_kernel, [VMEM] * 3,
        [shape(STRIPS, NEAR, *piece), shape(ROWS, NEAR, 128, 128)], (band, upper, u1),
    )
    u2, left, halos[2:] = lax.optimization_barrier((u2, left, halos[2:]))
    sizes = [min(RELAY, len(UPPER) - e) for e in range(0, len(UPPER), RELAY)]
    pieces = call(relay_kernel, [VMEM], [shape(n, *piece) for n in sizes], (u2,))
    pieces = [across(p, 1) for p in pieces]
    left = call(place_kernel, [VMEM] * 2, [shape(*left.shape)], (u2, left), aliases={1: 0})[0]
    both = [shape(*strips.shape), shape(*left.shape)]
    strips, left = call(
        complete_kernel, [VMEM] * (len(pieces) + 2), both, (*pieces, strips, left),
        aliases={len(pieces): 0, 1 + len(pieces): 1},
    )
    work = 2 * width * BAND * 128 * 128 * 32
    low, far, strips = call(
        low_kernel, [SMEM] + [VMEM] * 6,
        [shape(RADIUS, width, *piece), shape(len(FAR), width, *piece), both[0]],
        (kept, *halos, left, strips), flops=work * RADIUS, aliases={6: 2},
    )
    after = shifted(low, -1)
    close = call(
        high_kernel, [SMEM] + [VMEM] * 2, [shape(len(CLOSE), width, *piece)],
        (kept, strips, left), flops=work * (ROWS - RADIUS),
    )[0]
    close_in = shifted(close, 1)

    tables = (kept, cube)
    strips, partial = call(
        inner_kernel, [SMEM] * 2 + [VMEM] * 3,
        [shape(REACH, NEAR, *piece), shape(ROWS, slots, *piece, dtype=jnp.float32)],
        (*tables, low, close, left), flops=2 * slots * ROWS * ROWS * 128 * 128 * 32,
    )
    far, after, partial = lax.optimization_barrier((far, after, partial))
    far_in = shifted(far, 1)

    def rest(rows, start, places, halos, partial, strips):
        *own, strips = call(
            outer_kernel(rows, start, places, [p for p, _ in halos]), [SMEM] * 2 + [VMEM] * (3 + len(halos)),
            [shape(len(rows), share, *piece)] * 4 + [shape(*strips.shape)],
            (*tables, *(h for _, h in halos), left, partial, strips), aliases={4 + len(halos): 4}, free=True,
        )
        return [own[0], *(across(own[b], b) for b in (1, 2, 3))], strips

    late, strips = rest(LATE, 0, [*CLOSE, *AFTER], ((AFTER, after), (CLOSE, close_in)), partial, strips)
    partial = call(
        bridge_kernel, [SMEM] * 2 + [VMEM] * 3, [shape(len(EARLY), slots, *piece, dtype=jnp.float32)],
        (*tables, left, partial, strips), free=True,
    )[0]
    early, _ = rest(EARLY, EARLY[0], FAR, ((FAR, far_in),), partial, strips)

    result = shape(ROWS, share, 128, 128, dtype=jnp.float32)

    def scratch(rows):
        block = (len(rows), share, 128, 128)
        return [pltpu.VMEM(block, density.dtype), pltpu.VMEM(block, jnp.float32),
                pltpu.SemaphoreType.DMA((len(rows),))]

    out = call(
        final_kernel(LATE), [VMEM] * 4, [result], late,
        scratch(LATE), out_specs=[ANY],
    )[0]
    return call(
        final_kernel(EARLY), [VMEM] * 4 + [ANY], [result], (*early, out),
        scratch(EARLY), out_specs=[ANY], aliases={4: 0},
    )[0]


def solution(mesh):
    in_specs = (P(("row", "layer"), None, "col", None), P(), P(), P())
    out_specs = P(("row", "layer"), "col", None, None)
    return jax.shard_map(
        per_device, mesh=mesh, in_specs=in_specs, out_specs=out_specs, check_vma=False
    )
```

```python
import jax
import jax.numpy as jnp
from jax import lax
from jax.experimental import pallas as pl
from jax.experimental.pallas import tpu as pltpu
from jax.sharding import PartitionSpec as P

RADIUS = 5
BAND = 2 * RADIUS + 1
ROWS = 8
NEAR = ROWS + 2 * RADIUS
STRIPS = ROWS + 4 * RADIUS
REACH = ROWS + 6 * RADIUS
NT = (((1,), (1,)), ((), ()))
VMEM = pl.BlockSpec(memory_space=pltpu.VMEM)
SMEM = pl.BlockSpec(memory_space=pltpu.SMEM)
ANY = pl.BlockSpec(memory_space=pl.ANY)

SHIFTS = (1, -1, 2, -2)
OWN = [(j, o) for j in range(ROWS) for o in range(BAND)]
LISTS = (
    [(j, o) for j, o in OWN if ROWS <= j + o <= ROWS + RADIUS - 1],
    [(j, o) for j, o in OWN if RADIUS <= j + o <= 2 * RADIUS - 1],
    [(j, o) for j, o in OWN if j + o >= 2 * ROWS],
    [(j, o) for j, o in OWN if j + o < BAND - 1 - ROWS],
)
EDGES = (
    [(m, o) for m, o in OWN if m + o < RADIUS],
    [(m, o) for m, o in OWN if m + o >= RADIUS + ROWS],
)
UPPER = [(j, o) for j, o in OWN if o >= RADIUS or j + o < RADIUS]
LOWER = [(m, j) for m in range(ROWS) for j in range(m + 1, min(ROWS, m + RADIUS + 1))]
EARLY = range(0, 2 * RADIUS - ROWS)
LATE = range(2 * RADIUS - ROWS, ROWS)
AFTER = range(RADIUS + ROWS, NEAR)
CLOSE = range(2 * RADIUS - ROWS, RADIUS)
FAR = range(0, 2 * RADIUS - ROWS)
RELAY = 21


def own_place():
    group = lax.axis_index("row") * lax.axis_size("layer") + lax.axis_index("layer")
    return lax.axis_index("col"), group * ROWS


def wrapped(value, total):
    if total & (total - 1) == 0:
        return value & (total - 1)
    return jnp.where(value < 0, value + total, jnp.where(value >= total, value - total, value))


def reorder_kernel(pattern, density, h0, h1, h2, h3, upper, band):
    first, total = own_place()[1], pattern.shape[1]
    band[...] = jnp.zeros_like(band)
    for i in range(ROWS):
        for s in range(density.shape[1]):
            listed = pattern[s, first + i]
            o = wrapped(listed - (first + i) + RADIUS, total)
            band[i, jnp.where(listed >= 0, o, BAND)] = density[i, s]
    for out, entries in zip((h0, h1, h2, h3, upper), (*LISTS, UPPER)):
        for e, (j, o) in enumerate(entries):
            out[e] = band[j, o]


def place(left, piece, entries, col, b):
    start = pl.multiple_of((col ^ b) * 32, 32)
    for e, (i, o) in enumerate(entries):
        left[i, i + o, pl.ds(start, 32), :] = piece[e]


def prepare_kernel(band, upper, u1, strips, left):
    strips[...] = jnp.zeros_like(strips)
    left[...] = jnp.zeros_like(left)
    for i in range(ROWS):
        strips[i + 2 * RADIUS, i : i + BAND] = band[i, :BAND]
    col = own_place()[0]
    place(left, upper, UPPER, col, 0)
    place(left, u1, UPPER, col, 1)


def relay_kernel(u2, *pieces):
    for n, piece in enumerate(pieces):
        piece[...] = u2[n * RELAY : n * RELAY + piece.shape[0]]


def place_kernel(u2, left_in, left):
    del left_in
    place(left, u2, UPPER, own_place()[0], 2)


def complete_kernel(*refs):
    pieces, (strips, left) = refs[:-4], refs[-2:]
    col = own_place()[0]
    for n, piece in enumerate(pieces):
        place(left, piece, UPPER[n * RELAY : n * RELAY + piece.shape[0]], col, 3)
    shape = (32, 128)
    pick = lax.broadcasted_iota(jnp.int32, shape, 1) == lax.broadcasted_iota(jnp.int32, shape, 0) + col * 32
    pick = pick.astype(left.dtype)
    for edge in EDGES:
        blocks = jnp.concatenate([left[m, m + o] for m, o in edge], axis=0)
        turned = lax.dot_general(pick, blocks, NT, preferred_element_type=jnp.float32)
        for e, (m, o) in enumerate(edge):
            strips[m + o + RADIUS, m + RADIUS] = turned[:, e * 128 : (e + 1) * 128].astype(strips.dtype)
    for m, j in LOWER:
        left[j, m + RADIUS] = left[m, j + RADIUS].T


def gather_dot(strips, left, targets, i, places):
    w = jnp.concatenate([left[i, p] for p in places], axis=1)
    rows = [jnp.concatenate([strips[t, p] for p in places], axis=1) for t in targets]
    x = jnp.concatenate(rows, axis=0)
    return lax.dot_general(x, w, NT, preferred_element_type=jnp.float32)


def square_row(kept, strips, left, i, first):
    total = kept.shape[1]
    targets = [wrapped(kept[s, first + i] - first + 2 * RADIUS, total) for s in range(kept.shape[0])]
    acc = gather_dot(strips, left, targets, i, range(i, i + BAND))
    return acc.reshape(len(targets), 32, 128).astype(strips.dtype)


def low_kernel(kept, h0, h1, h2, h3, left, strips_in, low, far, strips, table, sem):
    del strips_in
    copy = pltpu.make_async_copy(kept, table, sem)
    copy.start()
    first = own_place()[1]
    for halo, entries, shift in zip((h0, h1, h2, h3), LISTS, SHIFTS):
        for e, (j, o) in enumerate(entries):
            row = j - shift * ROWS
            strips[row + 2 * RADIUS, row + o] = halo[e]
    copy.wait()
    for i in range(RADIUS):
        row = square_row(table, strips, left, i, first)
        low[i] = row
        if i >= ROWS - RADIUS:
            far[i - ROWS + RADIUS] = row


def high_kernel(kept, strips, left, close):
    for i in range(RADIUS, ROWS):
        close[i - RADIUS] = square_row(kept, strips, left, i, own_place()[1])


def strip_of(table, s, row, first):
    total = table.shape[1]
    return wrapped(table[s, wrapped(row, total)] - first + 3 * RADIUS, total)


def cube_targets(cube, i, col, first, share):
    return [strip_of(cube, (col ^ b) * share + q, first + i, first) for b in range(4) for q in range(share)]


def insert_rows(strips, kept, rows, places, first):
    for k, p in enumerate(places):
        for s in range(rows.shape[1]):
            strips[strip_of(kept, s, first - RADIUS + p, first), p] = rows[k, s]


def inner_kernel(kept, cube, low, close, left, strips, partial):
    col, first = own_place()
    strips[...] = jnp.zeros_like(strips)
    insert_rows(strips, kept, low, range(RADIUS, 2 * RADIUS), first)
    insert_rows(strips, kept, close, range(2 * RADIUS, RADIUS + ROWS), first)
    share = cube.shape[0] // 4

    @pl.loop(0, ROWS)
    def _(i):
        targets = cube_targets(cube, i, col, first, share)
        acc = gather_dot(strips, left, targets, i, range(RADIUS, RADIUS + ROWS))
        for e, t in enumerate(targets):
            mine = strips[t, i + RADIUS].astype(jnp.float32)
            partial[i, e] = 3.0 * mine - 2.0 * acc[e * 32 : (e + 1) * 32]


def bridge_kernel(kept, cube, left, partial, strips, early):
    share = cube.shape[0] // 4
    for n, i in enumerate(EARLY):
        targets = cube_targets(cube, i, *own_place(), share)
        acc = gather_dot(strips, left, targets, i, CLOSE)
        for e in range(len(targets)):
            early[n, e] = partial[i, e] - 2.0 * acc[e * 32 : (e + 1) * 32]


def outer_kernel(rows, start, places, arrived):
    def kernel(kept, cube, *refs):
        halos, (left, partial, _, o0, o1, o2, o3, strips, near, wanted, sems) = refs[:-11], refs[-11:]
        first_copy = pltpu.make_async_copy(kept, near, sems.at[0])
        second_copy = pltpu.make_async_copy(cube, wanted, sems.at[1])
        first_copy.start()
        second_copy.start()
        col, first = own_place()
        first_copy.wait()
        for halo, span in zip(halos, arrived):
            insert_rows(strips, near, halo, span, first)
        second_copy.wait()
        share = cube.shape[0] // 4
        for n, i in enumerate(rows):
            targets = cube_targets(wanted, i, col, first, share)
            acc = gather_dot(strips, left, targets, i, [p for p in places if i <= p < i + BAND])
            for e in range(len(targets)):
                piece = partial[i - start, e] - 2.0 * acc[e * 32 : (e + 1) * 32]
                (o0, o1, o2, o3)[e // share][n, e % share] = piece.astype(o0.dtype)

    return kernel


def final_kernel(rows):
    def kernel(*refs):
        col = own_place()[0]
        out, whole, turned, sems = refs[-4:]
        for b, p in enumerate(refs[:4]):
            whole[:, :, pl.ds(pl.multiple_of((col ^ b) * 32, 32), 32), :] = p[...]
        copies = []
        for n, i in enumerate(rows):
            for q in range(out.shape[1]):
                turned[n, q] = whole[n, q].T.astype(turned.dtype)
            copies.append(pltpu.make_async_copy(turned.at[n], out.at[i], sems.at[n]))
            copies[-1].start()
        for copy in copies:
            copy.wait()

    return kernel


def shape(*dims, dtype=jnp.bfloat16):
    return jax.ShapeDtypeStruct(dims, dtype)


def call(kernel, specs, outs, args, scratch=(), flops=0, aliases=None, out_specs=None, limit=16, free=False):
    size = sum(a.size * a.dtype.itemsize for a in args) + sum(o.size * o.dtype.itemsize for o in outs)
    size = 0 if free else size
    return pl.pallas_call(
        kernel,
        out_shape=outs,
        in_specs=specs,
        out_specs=out_specs or [VMEM] * len(outs),
        scratch_shapes=scratch,
        input_output_aliases=aliases or {},
        compiler_params=pltpu.CompilerParams(vmem_limit_bytes=limit << 20),
        cost_estimate=pl.CostEstimate(flops=flops, bytes_accessed=size, transcendentals=0),
    )(*args)


def per_device(density, pattern, square_filter, cube_filter):
    layers = lax.axis_size("layer")
    groups = lax.axis_size("row") * layers
    assert density.shape[0] == ROWS and lax.axis_size("col") == 4
    piece = density.shape[2:]
    pattern, kept, cube = pattern.T, square_filter.T, cube_filter.T
    width, slots = kept.shape[0], cube.shape[0]
    share = slots // 4

    def shifted(x, d):
        return lax.ppermute(x, ("row", "layer"), [(g, (g + d) % groups) for g in range(groups)])

    def across(x, bits):
        return lax.ppermute(x, "col", [(c, c ^ bits) for c in range(4)])

    *halos, upper, band = call(
        reorder_kernel, [SMEM, VMEM],
        [*(shape(len(e), *piece) for e in (*LISTS, UPPER)), shape(ROWS, BAND + 1, *piece)],
        (pattern, density),
    )
    u2 = across(upper, 2)
    u1 = across(upper, 1)
    halos = [shifted(p, d) for p, d in zip(halos, SHIFTS)]
    strips, left = call(
        prepare_kernel, [VMEM] * 3,
        [shape(STRIPS, NEAR, *piece), shape(ROWS, NEAR, 128, 128)], (band, upper, u1),
    )
    u2, left, halos[2:] = lax.optimization_barrier((u2, left, halos[2:]))
    sizes = [min(RELAY, len(UPPER) - e) for e in range(0, len(UPPER), RELAY)]
    pieces = call(relay_kernel, [VMEM], [shape(n, *piece) for n in sizes], (u2,))
    pieces = [across(p, 1) for p in pieces]
    left = call(place_kernel, [VMEM] * 2, [shape(*left.shape)], (u2, left), aliases={1: 0})[0]
    both = [shape(*strips.shape), shape(*left.shape)]
    strips, left = call(
        complete_kernel, [VMEM] * (len(pieces) + 2), both, (*pieces, strips, left),
        aliases={len(pieces): 0, 1 + len(pieces): 1},
    )
    work = 2 * width * BAND * 128 * 128 * 32
    low, far, strips = call(
        low_kernel, [ANY] + [VMEM] * 6,
        [shape(RADIUS, width, *piece), shape(len(FAR), width, *piece), both[0]],
        (kept, *halos, left, strips),
        [pltpu.SMEM(kept.shape, kept.dtype), pltpu.SemaphoreType.DMA], flops=work * RADIUS, aliases={6: 2},
    )
    after = shifted(low, -1)
    close = call(
        high_kernel, [SMEM] + [VMEM] * 2, [shape(len(CLOSE), width, *piece)],
        (kept, strips, left), flops=work * (ROWS - RADIUS),
    )[0]
    close_in = shifted(close, 1)

    tables = (kept, cube)
    strips, partial = call(
        inner_kernel, [SMEM] * 2 + [VMEM] * 3,
        [shape(REACH, NEAR, *piece), shape(ROWS, slots, *piece, dtype=jnp.float32)],
        (*tables, low, close, left), flops=2 * slots * ROWS * ROWS * 128 * 128 * 32,
    )
    far, after, partial = lax.optimization_barrier((far, after, partial))
    far_in = shifted(far, 1)

    def rest(rows, start, places, halos, partial, strips):
        *own, strips = call(
            outer_kernel(rows, start, places, [p for p, _ in halos]), [ANY] * 2 + [VMEM] * (3 + len(halos)),
            [shape(len(rows), share, *piece)] * 4 + [shape(*strips.shape)],
            (*tables, *(h for _, h in halos), left, partial, strips),
            [pltpu.SMEM(kept.shape, kept.dtype), pltpu.SMEM(cube.shape, cube.dtype), pltpu.SemaphoreType.DMA((2,))],
            aliases={4 + len(halos): 4}, free=True,
        )
        return [own[0], *(across(own[b], b) for b in (1, 2, 3))], strips

    late, strips = rest(LATE, 0, [*CLOSE, *AFTER], ((AFTER, after), (CLOSE, close_in)), partial, strips)
    partial = call(
        bridge_kernel, [SMEM] * 2 + [VMEM] * 3, [shape(len(EARLY), slots, *piece, dtype=jnp.float32)],
        (*tables, left, partial, strips), free=True,
    )[0]
    early, _ = rest(EARLY, EARLY[0], FAR, ((FAR, far_in),), partial, strips)

    result = shape(ROWS, share, 128, 128, dtype=jnp.float32)

    def scratch(rows):
        block = (len(rows), share, 128, 128)
        return [pltpu.VMEM(block, density.dtype), pltpu.VMEM(block, jnp.float32),
                pltpu.SemaphoreType.DMA((len(rows),))]

    out = call(
        final_kernel(LATE), [VMEM] * 4, [result], late,
        scratch(LATE), out_specs=[ANY],
    )[0]
    return call(
        final_kernel(EARLY), [VMEM] * 4 + [ANY], [result], (*early, out),
        scratch(EARLY), out_specs=[ANY], aliases={4: 0},
    )[0]


def solution(mesh):
    in_specs = (P(("row", "layer"), None, "col", None), P(), P(), P())
    out_specs = P(("row", "layer"), "col", None, None)
    return jax.shard_map(
        per_device, mesh=mesh, in_specs=in_specs, out_specs=out_specs, check_vma=False
    )
```

```python
import jax
import jax.numpy as jnp
from jax import lax
from jax.experimental import pallas as pl
from jax.experimental.pallas import tpu as pltpu
from jax.sharding import PartitionSpec as P

RADIUS = 5
BAND = 2 * RADIUS + 1
ROWS = 8
NEAR = ROWS + 2 * RADIUS
STRIPS = ROWS + 4 * RADIUS
REACH = ROWS + 6 * RADIUS
NT = (((1,), (1,)), ((), ()))
VMEM = pl.BlockSpec(memory_space=pltpu.VMEM)
SMEM = pl.BlockSpec(memory_space=pltpu.SMEM)
ANY = pl.BlockSpec(memory_space=pl.ANY)

SHIFTS = (1, -1, 2, -2)
OWN = [(j, o) for j in range(ROWS) for o in range(BAND)]
LISTS = (
    [(j, o) for j, o in OWN if ROWS <= j + o <= ROWS + RADIUS - 1],
    [(j, o) for j, o in OWN if RADIUS <= j + o <= 2 * RADIUS - 1],
    [(j, o) for j, o in OWN if j + o >= 2 * ROWS],
    [(j, o) for j, o in OWN if j + o < BAND - 1 - ROWS],
)
EDGES = (
    [(m, o) for m, o in OWN if m + o < RADIUS],
    [(m, o) for m, o in OWN if m + o >= RADIUS + ROWS],
)
UPPER = [(j, o) for j, o in OWN if o >= RADIUS or j + o < RADIUS]
LOWER = [(m, j) for m in range(ROWS) for j in range(m + 1, min(ROWS, m + RADIUS + 1))]
EARLY = range(0, 2 * RADIUS - ROWS)
LATE = range(2 * RADIUS - ROWS, ROWS)
AFTER = range(RADIUS + ROWS, NEAR)
CLOSE = range(2 * RADIUS - ROWS, RADIUS)
FAR = range(0, 2 * RADIUS - ROWS)
RELAY = 21


def own_place():
    group = lax.axis_index("row") * lax.axis_size("layer") + lax.axis_index("layer")
    return lax.axis_index("col"), group * ROWS


def wrapped(value, total):
    if total & (total - 1) == 0:
        return value & (total - 1)
    return jnp.where(value < 0, value + total, jnp.where(value >= total, value - total, value))


def reorder_kernel(pattern, density, h0, h1, h2, h3, upper, band, blocks, table, sems):
    first, total = own_place()[1], pattern.shape[1]
    copies = [pltpu.make_async_copy(density.at[i], blocks.at[i], sems.at[i]) for i in range(ROWS)]
    listing = pltpu.make_async_copy(pattern, table, sems.at[ROWS])
    for copy in (listing, *copies):
        copy.start()
    band[...] = jnp.zeros_like(band)
    listing.wait()
    for i in range(ROWS):
        copies[i].wait()
        for s in range(blocks.shape[1]):
            listed = table[s, first + i]
            o = wrapped(listed - (first + i) + RADIUS, total)
            band[i, jnp.where(listed >= 0, o, BAND)] = blocks[i, s]
    for out, entries in zip((h0, h1, h2, h3, upper), (*LISTS, UPPER)):
        for e, (j, o) in enumerate(entries):
            out[e] = band[j, o]


def place(left, piece, entries, col, b):
    start = pl.multiple_of((col ^ b) * 32, 32)
    for e, (i, o) in enumerate(entries):
        left[i, i + o, pl.ds(start, 32), :] = piece[e]


def prepare_kernel(band, upper, u1, strips, left):
    strips[...] = jnp.zeros_like(strips)
    left[...] = jnp.zeros_like(left)
    for i in range(ROWS):
        strips[i + 2 * RADIUS, i : i + BAND] = band[i, :BAND]
    col = own_place()[0]
    place(left, upper, UPPER, col, 0)
    place(left, u1, UPPER, col, 1)


def relay_kernel(u2, *pieces):
    for n, piece in enumerate(pieces):
        piece[...] = u2[n * RELAY : n * RELAY + piece.shape[0]]


def place_kernel(u2, left_in, left):
    del left_in
    place(left, u2, UPPER, own_place()[0], 2)


def complete_kernel(*refs):
    pieces, (strips, left) = refs[:-4], refs[-2:]
    col = own_place()[0]
    for n, piece in enumerate(pieces):
        place(left, piece, UPPER[n * RELAY : n * RELAY + piece.shape[0]], col, 3)
    shape = (32, 128)
    pick = lax.broadcasted_iota(jnp.int32, shape, 1) == lax.broadcasted_iota(jnp.int32, shape, 0) + col * 32
    pick = pick.astype(left.dtype)
    for edge in EDGES:
        blocks = jnp.concatenate([left[m, m + o] for m, o in edge], axis=0)
        turned = lax.dot_general(pick, blocks, NT, preferred_element_type=jnp.float32)
        for e, (m, o) in enumerate(edge):
            strips[m + o + RADIUS, m + RADIUS] = turned[:, e * 128 : (e + 1) * 128].astype(strips.dtype)
    for m, j in LOWER:
        left[j, m + RADIUS] = left[m, j + RADIUS].T


def gather_dot(strips, left, targets, i, places):
    w = jnp.concatenate([left[i, p] for p in places], axis=1)
    rows = [jnp.concatenate([strips[t, p] for p in places], axis=1) for t in targets]
    x = jnp.concatenate(rows, axis=0)
    return lax.dot_general(x, w, NT, preferred_element_type=jnp.float32)


def square_row(kept, strips, left, i, first):
    total = kept.shape[1]
    targets = [wrapped(kept[s, first + i] - first + 2 * RADIUS, total) for s in range(kept.shape[0])]
    acc = gather_dot(strips, left, targets, i, range(i, i + BAND))
    return acc.reshape(len(targets), 32, 128).astype(strips.dtype)


def low_kernel(kept, h0, h1, h2, h3, left, strips_in, low, far, strips, table, sem):
    del strips_in
    copy = pltpu.make_async_copy(kept, table, sem)
    copy.start()
    first = own_place()[1]
    for halo, entries, shift in zip((h0, h1, h2, h3), LISTS, SHIFTS):
        for e, (j, o) in enumerate(entries):
            row = j - shift * ROWS
            strips[row + 2 * RADIUS, row + o] = halo[e]
    copy.wait()
    for i in range(RADIUS):
        row = square_row(table, strips, left, i, first)
        low[i] = row
        if i >= ROWS - RADIUS:
            far[i - ROWS + RADIUS] = row


def high_kernel(kept, strips, left, close):
    for i in range(RADIUS, ROWS):
        close[i - RADIUS] = square_row(kept, strips, left, i, own_place()[1])


def strip_of(table, s, row, first):
    total = table.shape[1]
    return wrapped(table[s, wrapped(row, total)] - first + 3 * RADIUS, total)


def cube_targets(cube, i, col, first, share):
    return [strip_of(cube, (col ^ b) * share + q, first + i, first) for b in range(4) for q in range(share)]


def insert_rows(strips, kept, rows, places, first):
    for k, p in enumerate(places):
        for s in range(rows.shape[1]):
            strips[strip_of(kept, s, first - RADIUS + p, first), p] = rows[k, s]


def inner_kernel(kept, cube, low, close, left, strips, partial):
    col, first = own_place()
    strips[...] = jnp.zeros_like(strips)
    insert_rows(strips, kept, low, range(RADIUS, 2 * RADIUS), first)
    insert_rows(strips, kept, close, range(2 * RADIUS, RADIUS + ROWS), first)
    share = cube.shape[0] // 4

    @pl.loop(0, ROWS)
    def _(i):
        targets = cube_targets(cube, i, col, first, share)
        acc = gather_dot(strips, left, targets, i, range(RADIUS, RADIUS + ROWS))
        for e, t in enumerate(targets):
            mine = strips[t, i + RADIUS].astype(jnp.float32)
            partial[i, e] = 3.0 * mine - 2.0 * acc[e * 32 : (e + 1) * 32]


def bridge_kernel(kept, cube, left, partial, strips, early):
    share = cube.shape[0] // 4
    for n, i in enumerate(EARLY):
        targets = cube_targets(cube, i, *own_place(), share)
        acc = gather_dot(strips, left, targets, i, CLOSE)
        for e in range(len(targets)):
            early[n, e] = partial[i, e] - 2.0 * acc[e * 32 : (e + 1) * 32]


def outer_kernel(rows, start, places, arrived):
    def kernel(kept, cube, *refs):
        halos, (left, partial, _, o0, o1, o2, o3, strips, near, wanted, sems) = refs[:-11], refs[-11:]
        first_copy = pltpu.make_async_copy(kept, near, sems.at[0])
        second_copy = pltpu.make_async_copy(cube, wanted, sems.at[1])
        first_copy.start()
        second_copy.start()
        col, first = own_place()
        first_copy.wait()
        for halo, span in zip(halos, arrived):
            insert_rows(strips, near, halo, span, first)
        second_copy.wait()
        share = cube.shape[0] // 4
        for n, i in enumerate(rows):
            targets = cube_targets(wanted, i, col, first, share)
            acc = gather_dot(strips, left, targets, i, [p for p in places if i <= p < i + BAND])
            for e in range(len(targets)):
                piece = partial[i - start, e] - 2.0 * acc[e * 32 : (e + 1) * 32]
                (o0, o1, o2, o3)[e // share][n, e % share] = piece.astype(o0.dtype)

    return kernel


def final_kernel(rows):
    def kernel(*refs):
        col = own_place()[0]
        out, whole, turned, sems = refs[-4:]
        for b, p in enumerate(refs[:4]):
            whole[:, :, pl.ds(pl.multiple_of((col ^ b) * 32, 32), 32), :] = p[...]
        copies = []
        for n, i in enumerate(rows):
            for q in range(out.shape[1]):
                turned[n, q] = whole[n, q].T.astype(turned.dtype)
            copies.append(pltpu.make_async_copy(turned.at[n], out.at[i], sems.at[n]))
            copies[-1].start()
        for copy in copies:
            copy.wait()

    return kernel


def shape(*dims, dtype=jnp.bfloat16):
    return jax.ShapeDtypeStruct(dims, dtype)


def call(kernel, specs, outs, args, scratch=(), flops=0, aliases=None, out_specs=None, limit=16, free=False):
    size = sum(a.size * a.dtype.itemsize for a in args) + sum(o.size * o.dtype.itemsize for o in outs)
    size = 0 if free else size
    return pl.pallas_call(
        kernel,
        out_shape=outs,
        in_specs=specs,
        out_specs=out_specs or [VMEM] * len(outs),
        scratch_shapes=scratch,
        input_output_aliases=aliases or {},
        compiler_params=pltpu.CompilerParams(vmem_limit_bytes=limit << 20),
        cost_estimate=pl.CostEstimate(flops=flops, bytes_accessed=size, transcendentals=0),
    )(*args)


def per_device(density, pattern, square_filter, cube_filter):
    layers = lax.axis_size("layer")
    groups = lax.axis_size("row") * layers
    assert density.shape[0] == ROWS and lax.axis_size("col") == 4
    piece = density.shape[2:]
    pattern, kept, cube = pattern.T, square_filter.T, cube_filter.T
    width, slots = kept.shape[0], cube.shape[0]
    share = slots // 4

    def shifted(x, d):
        return lax.ppermute(x, ("row", "layer"), [(g, (g + d) % groups) for g in range(groups)])

    def across(x, bits):
        return lax.ppermute(x, "col", [(c, c ^ bits) for c in range(4)])

    *halos, upper, band = call(
        reorder_kernel, [ANY, ANY],
        [*(shape(len(e), *piece) for e in (*LISTS, UPPER)), shape(ROWS, BAND + 1, *piece)],
        (pattern, density),
        [pltpu.VMEM(density.shape, density.dtype), pltpu.SMEM(pattern.shape, pattern.dtype),
         pltpu.SemaphoreType.DMA((ROWS + 1,))], limit=60,
    )
    u2 = across(upper, 2)
    u1 = across(upper, 1)
    halos = [shifted(p, d) for p, d in zip(halos, SHIFTS)]
    strips, left = call(
        prepare_kernel, [VMEM] * 3,
        [shape(STRIPS, NEAR, *piece), shape(ROWS, NEAR, 128, 128)], (band, upper, u1),
    )
    u2, left, halos[2:] = lax.optimization_barrier((u2, left, halos[2:]))
    sizes = [min(RELAY, len(UPPER) - e) for e in range(0, len(UPPER), RELAY)]
    pieces = call(relay_kernel, [VMEM], [shape(n, *piece) for n in sizes], (u2,))
    pieces = [across(p, 1) for p in pieces]
    left = call(place_kernel, [VMEM] * 2, [shape(*left.shape)], (u2, left), aliases={1: 0})[0]
    both = [shape(*strips.shape), shape(*left.shape)]
    strips, left = call(
        complete_kernel, [VMEM] * (len(pieces) + 2), both, (*pieces, strips, left),
        aliases={len(pieces): 0, 1 + len(pieces): 1},
    )
    work = 2 * width * BAND * 128 * 128 * 32
    low, far, strips = call(
        low_kernel, [ANY] + [VMEM] * 6,
        [shape(RADIUS, width, *piece), shape(len(FAR), width, *piece), both[0]],
        (kept, *halos, left, strips),
        [pltpu.SMEM(kept.shape, kept.dtype), pltpu.SemaphoreType.DMA], flops=work * RADIUS, aliases={6: 2},
    )
    after = shifted(low, -1)
    close = call(
        high_kernel, [SMEM] + [VMEM] * 2, [shape(len(CLOSE), width, *piece)],
        (kept, strips, left), flops=work * (ROWS - RADIUS),
    )[0]
    close_in = shifted(close, 1)

    tables = (kept, cube)
    strips, partial = call(
        inner_kernel, [SMEM] * 2 + [VMEM] * 3,
        [shape(REACH, NEAR, *piece), shape(ROWS, slots, *piece, dtype=jnp.float32)],
        (*tables, low, close, left), flops=2 * slots * ROWS * ROWS * 128 * 128 * 32,
    )
    far, after, partial = lax.optimization_barrier((far, after, partial))
    far_in = shifted(far, 1)

    def rest(rows, start, places, halos, partial, strips):
        *own, strips = call(
            outer_kernel(rows, start, places, [p for p, _ in halos]), [ANY] * 2 + [VMEM] * (3 + len(halos)),
            [shape(len(rows), share, *piece)] * 4 + [shape(*strips.shape)],
            (*tables, *(h for _, h in halos), left, partial, strips),
            [pltpu.SMEM(kept.shape, kept.dtype), pltpu.SMEM(cube.shape, cube.dtype), pltpu.SemaphoreType.DMA((2,))],
            aliases={4 + len(halos): 4}, free=True,
        )
        return [own[0], *(across(own[b], b) for b in (1, 2, 3))], strips

    late, strips = rest(LATE, 0, [*CLOSE, *AFTER], ((AFTER, after), (CLOSE, close_in)), partial, strips)
    partial = call(
        bridge_kernel, [SMEM] * 2 + [VMEM] * 3, [shape(len(EARLY), slots, *piece, dtype=jnp.float32)],
        (*tables, left, partial, strips), free=True,
    )[0]
    early, _ = rest(EARLY, EARLY[0], FAR, ((FAR, far_in),), partial, strips)

    result = shape(ROWS, share, 128, 128, dtype=jnp.float32)

    def scratch(rows):
        block = (len(rows), share, 128, 128)
        return [pltpu.VMEM(block, density.dtype), pltpu.VMEM(block, jnp.float32),
                pltpu.SemaphoreType.DMA((len(rows),))]

    out = call(
        final_kernel(LATE), [VMEM] * 4, [result], late,
        scratch(LATE), out_specs=[ANY],
    )[0]
    return call(
        final_kernel(EARLY), [VMEM] * 4 + [ANY], [result], (*early, out),
        scratch(EARLY), out_specs=[ANY], aliases={4: 0},
    )[0]


def solution(mesh):
    in_specs = (P(("row", "layer"), None, "col", None), P(), P(), P())
    out_specs = P(("row", "layer"), "col", None, None)
    return jax.shard_map(
        per_device, mesh=mesh, in_specs=in_specs, out_specs=out_specs, check_vma=False
    )
```
